512 devices in a mesh: ctx: 32 (over y_lo, z), roll: 16 (over x, y_hi, core).
Axes of the slice: x: 4, y: 8 (y_hi: 2, y_lo: 4; y = y_hi * 4 + y_lo), z: 8, core: 2. Of those that a mesh axis runs over, the one named last changes fastest.
Arguments:
- block_order: int32 [32], replicated, may hold values from 0 to 31, as said below
- segment_ids: int32 [4096], replicated, may hold values from 0 to 3, as said below
- layer_input: bfloat16 [8192, 4096], P(None, 'ctx'), may hold values from -6 to 6
- query_states: bfloat16 [4096, 768], P('ctx')
- key_states: bfloat16 [4096, 128], P('ctx')
- value_states: bfloat16 [4096, 128], P('ctx'), may hold values from -6 to 6
- out_grad: bfloat16 [4096, 768], P('ctx'), may hold values from -24 to 24
- master_weight: float32 [8192, 128], P(('ctx', 'roll')), may hold values from -0.0625 to 0.0625
- first_moment: float32 [8192, 128], P(('ctx', 'roll')), may hold values from -60 to 60
- second_moment: float32 [8192, 128], P(('ctx', 'roll')), may hold values from 30 to 3000
Outputs:
- query_grad: bfloat16 [4096, 768], P('ctx')
- key_value_grad: bfloat16 [4096, 256], P('ctx')
- updated_master: float32 [8192, 128], P(('ctx', 'roll'))
- updated_first: float32 [8192, 128], P(('ctx', 'roll'))
- updated_second: float32 [8192, 128], P(('ctx', 'roll'))
- rollout_weight: bfloat16 [8192, 128], P('ctx')
The draws below stay inside these ranges and needn't reach their ends.
Inputs may be any that keep to these rules, and one draw needn't show every extreme that they name: A permutation: index c of ctx holds the tokens at positions block_order[c] * 128 to block_order[c] * 128 + 127, in order; every block is held once. `segment_ids`: ids never fall along sequence positions; there are exactly 4 rollouts; no rollout begins at offset 128 // 2 of a block.
All inputs are finite; a program needn't handle non-finite values.
Results may differ from the reference program's by a relative error of at most 0.028.
Values may be sent and summed in bfloat16 or wider, within the bound.
A program may use at most 64 MiB of HBM per device.

```python
import math
import jax
import jax.numpy as jnp
from jax import lax

D = 8192
HD = 128
GROUP = 6
NSEG = 4
ROWS = 128
SEQ = 4096
N_CTX = 32


def plan_order(key):
    return jax.random.permutation(jax.random.fold_in(key, 11), N_CTX).astype(jnp.int32)


def draw_block_order(key, part):
    return plan_order(key)


def draw_segment_ids(key, part):
    block_seq = plan_order(key)
    blocks = jax.random.permutation(jax.random.fold_in(key, 12), N_CTX)[:NSEG - 1].astype(jnp.int32)
    offsets = jax.random.randint(jax.random.fold_in(key, 13), (NSEG - 1,), 1, ROWS, dtype=jnp.int32)
    offsets = jnp.where(offsets == ROWS // 2, ROWS // 2 + 1, offsets)
    starts = blocks * ROWS + offsets
    cut_flags = jnp.zeros((SEQ,), jnp.int32).at[starts].set(1)
    in_order = jnp.cumsum(cut_flags).astype(jnp.int32)
    row_positions = (block_seq[:, None] * ROWS + jnp.arange(ROWS, dtype=jnp.int32)[None, :]).reshape(-1)
    return in_order[row_positions]


def draw_key_states(key, part):
    sample = jnp.clip(jax.random.normal(jax.random.fold_in(key, 41), (SEQ, HD), jnp.float32), -5.0, 5.0)
    return sample.astype(jnp.bfloat16)


def draw_query_states(key, part):
    sample = jnp.clip(jax.random.normal(jax.random.fold_in(key, 51), (SEQ, GROUP * HD), jnp.float32), -5.0, 5.0)
    return sample.astype(jnp.bfloat16)


def raised(values, rng, source, target, parts, factor):
    owner, partner = [(jnp.arange(values.shape[dim]) // (values.shape[dim] // parts)).reshape([-1 if axis == dim else 1 for axis in range(values.ndim)]) for dim in (source, target)]
    chosen = jax.random.permutation(rng, parts)[partner]
    strong = (owner == chosen) | (owner == (partner + parts // 2) % parts)
    return jnp.where(strong, factor * values, values)


def block_levels(own_key, extent, cuts, smallest, high):
    level, own = 1.0, jax.random.fold_in(own_key, 6)
    for position, shards_of in cuts:
        steps = jnp.exp(jax.random.uniform(jax.random.fold_in(own, position), (shards_of,), jnp.float32, smallest / len(cuts), high / len(cuts)))
        level = level * jnp.repeat(steps, extent[position] // shards_of).reshape([-1 if axis == position else 1 for axis in range(len(extent))])
    return level


def gaussian(own_key, extent, scale, limit, split=(), kind=jnp.bfloat16):
    result = scale * jax.random.normal(own_key, extent, jnp.float32)
    if split:
        result = result * block_levels(own_key, extent, split, -0.22, 0.18)
    return jnp.clip(result, -limit, limit).astype(kind)


def heavy_noise(stream_key, dims, deviation, most, shards, heavy, held_as=jnp.bfloat16):
    values = deviation * jax.random.normal(stream_key, dims, jnp.float32)
    if shards:
        values = values * block_levels(stream_key, dims, shards, -0.22, 0.18)
    return jnp.clip(raised(values, jax.random.fold_in(stream_key, 3), *heavy), -most, most).astype(held_as)


def setup_inputs(seed: int = 0) -> dict:
    splits = jax.random.split(jax.random.key(seed), 11)
    return {
        "block_order": draw_block_order(jax.random.fold_in(splits[10], 71), 0),
        "segment_ids": draw_segment_ids(jax.random.fold_in(splits[10], 71), 0),
        "layer_input": heavy_noise(splits[2], (D, SEQ), 1.0, 6.0, ((1, 32),), (1, 0, 32, 2.75)),
        "query_states": draw_query_states(jax.random.fold_in(splits[10], 71), 0),
        "key_states": draw_key_states(jax.random.fold_in(splits[10], 71), 0),
        "value_states": gaussian(splits[5], (SEQ, HD), 1.0, 6.0, ((0, 32),)),
        "out_grad": gaussian(splits[6], (SEQ, GROUP * HD), 4.0, 24.0, ((0, 32),)),
        "master_weight": gaussian(splits[7], (D, HD), D ** -0.5, 0.0625, ((0, 512),), jnp.float32),
        "first_moment": gaussian(splits[8], (D, HD), 10.0, 60.0, ((0, 512),), jnp.float32),
        "second_moment": jnp.clip(jnp.exp(math.log(3000.0) - 4.6051702 * jax.random.uniform(splits[9], (D, HD), jnp.float32) ** block_levels(splits[9], (D, HD), ((0, 512),), -0.2, 0.2)), 30.0, 3000.0),
    }


NEG_FILL = -1e+30
BETA_ONE = 0.9
BETA_TWO = 0.95
ADAM_EPS = 1e-08
DECAY_RATE = 0.1
LEARN_RATE = 1e-06
CORRECT_ONE = 0.9999734386011124
CORRECT_TWO = 0.994079470779666

def reference(block_order, segment_ids, layer_input, query_states, key_states, value_states, out_grad, master_weight, first_moment, second_moment):
    score_scale = HD ** (-0.5)
    offsets = jnp.arange(ROWS, dtype=jnp.int32)
    positions = (block_order[:, None] * ROWS + offsets[None, :]).reshape(-1)
    query_blocks = query_states.reshape(N_CTX, ROWS * GROUP, HD)
    grad_blocks = out_grad.reshape(N_CTX, ROWS * GROUP, HD)
    pos_blocks = positions.reshape(N_CTX, ROWS)
    seg_blocks = segment_ids.reshape(N_CTX, ROWS)

    def one_block(carry, inputs):
        q_rows, do_rows, q_pos, q_seg = inputs
        visible = (positions[None, :] <= q_pos[:, None]) & (segment_ids[None, :] == q_seg[:, None])
        visible = jnp.repeat(visible, GROUP, axis=0)
        scores = jnp.dot(q_rows, key_states.T, preferred_element_type=jnp.float32) * score_scale
        scores = jnp.where(visible, scores, NEG_FILL)
        row_top = lax.optimization_barrier(jnp.max(scores, axis=1, keepdims=True))
        expo = jnp.where(visible, jnp.exp(scores - row_top), 0.0)
        log_total = row_top + jnp.log(lax.optimization_barrier(jnp.sum(expo, axis=1, keepdims=True)))
        weights = jnp.where(visible, jnp.exp(scores - log_total), 0.0)
        dprob = jnp.dot(do_rows, value_states.T, preferred_element_type=jnp.float32)
        delta = lax.optimization_barrier(jnp.sum(weights * dprob, axis=1, keepdims=True))
        dscore = weights * (dprob - delta)
        weights_half = weights.astype(jnp.bfloat16)
        dscore_half = dscore.astype(jnp.bfloat16)
        query_part = jnp.dot(dscore_half, key_states, preferred_element_type=jnp.float32) * score_scale
        key_part = jnp.dot(dscore_half.T, q_rows, preferred_element_type=jnp.float32) * score_scale
        value_part = jnp.dot(weights_half.T, do_rows, preferred_element_type=jnp.float32)
        part_half = lax.optimization_barrier(jnp.concatenate([key_part, value_part], axis=1).astype(jnp.bfloat16))
        return (carry + part_half.astype(jnp.float32), query_part.astype(jnp.bfloat16))
    kv_sum, query_parts = lax.scan(one_block, jnp.zeros((SEQ, 2 * HD), jnp.float32), (query_blocks, grad_blocks, pos_blocks, seg_blocks))
    query_grad = query_parts.reshape(SEQ, GROUP * HD)
    key_value_grad = kv_sum.astype(jnp.bfloat16)
    input_blocks = layer_input.reshape(D, N_CTX, ROWS).transpose(1, 0, 2)
    grad_rows = key_value_grad[:, :HD].reshape(N_CTX, ROWS, HD)

    def weight_block(carry, inputs):
        x_block, g_block = inputs
        part = lax.optimization_barrier(jnp.dot(x_block, g_block, preferred_element_type=jnp.float32).astype(jnp.bfloat16))
        return (carry + part.astype(jnp.float32), 0.0)
    weight_grad, unused = lax.scan(weight_block, jnp.zeros((D, HD), jnp.float32), (input_blocks, grad_rows))
    updated_first = BETA_ONE * first_moment + (1.0 - BETA_ONE) * weight_grad
    updated_second = BETA_TWO * second_moment + (1.0 - BETA_TWO) * weight_grad * weight_grad
    update = updated_first / CORRECT_ONE / (jnp.sqrt(updated_second / CORRECT_TWO) + ADAM_EPS) + DECAY_RATE * master_weight
    updated_master = master_weight - LEARN_RATE * update
    rollout_weight = updated_master.astype(jnp.bfloat16)
    return (query_grad, key_value_grad, updated_master, updated_first, updated_second, rollout_weight)
```

```python
import functools

import jax
import jax.numpy as jnp
from jax import lax
from jax.experimental import pallas as pl
from jax.experimental.pallas import tpu as pltpu
from jax.sharding import PartitionSpec as P

NEG_FILL = -1e30
BETA_ONE = 0.9
BETA_TWO = 0.95
ADAM_EPS = 1e-08
DECAY_RATE = 0.1
LEARN_RATE = 1e-06
CORRECT_ONE = 0.9999734386011124
CORRECT_TWO = 0.994079470779666

MESH = pl.DeviceIdType.MESH
SHARE = 8
OWN = 16
HEADS = 6
BF = jnp.bfloat16
F32 = jnp.float32

(LOAD, KV, STATS, DKV, DQ, DQALL, KVG, WG, ROLL, OUT) = range(10)


def push(axis, me, count, src, dst, send_sem, recv_sem):
    @pl.loop(1, count)
    def _(step):
        peer = lax.rem(me + step, count)
        pltpu.make_async_remote_copy(
            src_ref=src(peer),
            dst_ref=dst,
            send_sem=send_sem,
            recv_sem=recv_sem,
            device_id={axis: peer},
            device_id_type=MESH,
        ).start()


def drain(buf, count, sem):
    part = buf.at[pl.ds(0, count - 1)]
    pltpu.make_async_copy(part, part, sem).wait()


def contract(left, right, dims):
    return lax.dot_general(left, right, (dims, ((), ())), preferred_element_type=F32)


def kernel(
    ctx,
    roll,
    order_hbm,
    seg_hbm,
    x_hbm,
    q_hbm,
    k_hbm,
    v_hbm,
    do_hbm,
    mw_hbm,
    m1_hbm,
    m2_hbm,
    qg_out,
    kvg_out,
    mw_out,
    m1_out,
    m2_out,
    rw_out,
    order,
    seg,
    x_in,
    q_in,
    k_in,
    v_in,
    do_in,
    mw_in,
    m1_in,
    m2_in,
    kv_wide,
    bias,
    expo,
    dprob,
    kv,
    stats,
    dkv_to,
    dkv_from,
    dq_to,
    dq_from,
    dq_all,
    kvg,
    wg_to,
    wg_from,
    rolled,
    qg_stage,
    kvg_stage,
    mw_stage,
    m1_stage,
    m2_stage,
    load_sem,
    send_sem,
    recv_sem,
    out_sem,
):
    c = lax.axis_index("ctx")
    r = lax.axis_index("roll")
    rows = k_in.shape[0]
    hd = k_in.shape[1]
    keys = ctx * SHARE
    scale = hd**-0.5
    piece = HEADS * SHARE

    loads = [
        pltpu.make_async_copy(src, dst, load_sem.at[i])
        for i, (src, dst) in enumerate(
            (
                (k_hbm, k_in),
                (v_hbm, v_in),
                (order_hbm, order),
                (seg_hbm, seg),
                (q_hbm, q_in),
                (do_hbm, do_in),
                (x_hbm.at[:, r], x_in),
                (mw_hbm, mw_in),
                (m1_hbm, m1_in),
                (m2_hbm, m2_in),
            )
        )
    ]
    for load in loads:
        load.start()

    barrier = pltpu.get_barrier_semaphore()

    @pl.loop(1, ctx)
    def _(step):
        pl.semaphore_signal(
            barrier, inc=1, device_id={"ctx": lax.rem(c + step, ctx)}, device_id_type=MESH
        )

    @pl.loop(1, roll)
    def _(step):
        pl.semaphore_signal(
            barrier, inc=1, device_id={"roll": lax.rem(r + step, roll)}, device_id_type=MESH
        )

    loads[0].wait()
    loads[1].wait()
    kv_wide[0] = k_in[...].astype(F32)
    kv_wide[1] = v_in[...].astype(F32)
    first = pl.multiple_of(r * SHARE, SHARE)
    own = jnp.concatenate(
        [kv_wide[0, pl.ds(first, SHARE), :], kv_wide[1, pl.ds(first, SHARE), :]], axis=0
    )
    kv[c] = own.astype(BF)
    pl.semaphore_wait(barrier, ctx + roll - 2)
    push("ctx", c, ctx, lambda peer: kv.at[c], kv.at[c], send_sem.at[KV], recv_sem.at[KV])

    loads[2].wait()
    loads[3].wait()
    ids = seg[...]
    q_seg = seg[pl.ds(c, 1), :]
    lane = lax.broadcasted_iota(jnp.int32, (1, rows), 1)
    q_pos = order[c] * rows + lane
    start = jnp.zeros((1, rows), F32)
    for rollout in range(3):
        total = jnp.sum(jnp.where(ids == rollout, 1.0, 0.0), axis=0, keepdims=True)
        total = jnp.sum(total, axis=1, keepdims=True)
        start = start + jnp.where(q_seg > rollout, total, 0.0)
    start = start.astype(jnp.int32)
    sub = lax.broadcasted_iota(jnp.int32, (SHARE, rows), 0)
    latest = q_pos - sub - r * SHARE
    earliest = start - sub - r * SHARE
    for block in range(ctx):
        base = order[block] * rows
        seen = (latest >= base) & (earliest <= base)
        bias[pl.ds(block * SHARE, SHARE), :] = jnp.where(seen, 0.0, NEG_FILL)

    loads[4].wait()
    loads[5].wait()
    drain(kv, ctx, recv_sem.at[KV])
    wide = kv[...].astype(F32)
    key = wide[:, :SHARE, :].reshape(keys, hd).astype(BF)
    value = wide[:, SHARE:, :].reshape(keys, hd).astype(BF)
    tops, sums, weighteds = [], [], []
    for h in range(HEADS):
        cols = pl.ds(h * hd, hd)
        scores = contract(key, q_in[:, cols], ((1,), (1,))) * scale + bias[...]
        grads = contract(value, do_in[:, cols], ((1,), (1,)))
        top = jnp.max(scores, axis=0, keepdims=True)
        weights = jnp.exp(scores - top)
        expo[h] = weights
        dprob[h] = grads
        tops.append(top)
        sums.append(jnp.sum(weights, axis=0, keepdims=True))
        weighteds.append(jnp.sum(weights * grads, axis=0, keepdims=True))
    pad = jnp.zeros((8 - HEADS, rows), F32)
    for i, parts in enumerate((tops, sums, weighteds)):
        stats[r, i] = jnp.concatenate([*parts, pad], axis=0)
    push(
        "roll", r, roll, lambda peer: stats.at[r], stats.at[r], send_sem.at[STATS], recv_sem.at[STATS]
    )
    own_top = stats[r, 0]
    drain(stats, roll, recv_sem.at[STATS])
    top = jnp.max(stats[:, 0], axis=0)
    factor = jnp.exp(stats[:, 0] - top[None])
    total = jnp.sum(stats[:, 1] * factor, axis=0)
    delta = jnp.sum(stats[:, 2] * factor, axis=0) / total
    norm = jnp.exp(own_top - top) / total

    key_grad = jnp.zeros((keys, hd), F32)
    value_grad = jnp.zeros((keys, hd), F32)
    halves = []
    for h in range(HEADS):
        cols = pl.ds(h * hd, hd)
        prob = expo[h] * norm[h : h + 1]
        dscore = (prob * (dprob[h] - delta[h : h + 1])).astype(BF)
        halves.append(dscore)
        key_grad += contract(dscore, q_in[:, cols], ((1,), (0,)))
        value_grad += contract(prob.astype(BF), do_in[:, cols], ((1,), (0,)))
    both = jnp.concatenate(
        [(key_grad * scale).reshape(ctx, SHARE, hd), value_grad.reshape(ctx, SHARE, hd)], axis=1
    )
    dkv_to[...] = both.astype(BF)
    push(
        "ctx", c, ctx, lambda peer: dkv_to.at[peer], dkv_from.at[c], send_sem.at[DKV], recv_sem.at[DKV]
    )
    dkv_from[c] = dkv_to[c]

    query_parts = [contract(half, key, ((0,), (0,))) for half in halves]
    dq_to[...] = jnp.concatenate(query_parts, axis=0).astype(BF).reshape(roll, piece, hd)
    push(
        "roll", r, roll, lambda peer: dq_to.at[peer], dq_from.at[r], send_sem.at[DQ], recv_sem.at[DQ]
    )
    dq_from[r] = dq_to[r]

    drain(dkv_from, ctx, recv_sem.at[DKV])
    kvg[r] = jnp.sum(dkv_from[...].astype(F32), axis=0).astype(BF)
    push("roll", r, roll, lambda peer: kvg.at[r], kvg.at[r], send_sem.at[KVG], recv_sem.at[KVG])
    loads[6].wait()
    drain(kvg, roll, recv_sem.at[KVG])
    wide = kvg[...].astype(F32)
    kv_wide[0] = wide[:, :SHARE, :].reshape(rows, hd)
    kv_wide[1] = wide[:, SHARE:, :].reshape(rows, hd)
    key_grad = kv_wide[0].astype(BF)
    product = contract(x_in[...].reshape(ctx * OWN, rows), key_grad, ((1,), (0,)))
    wg_to[...] = product.astype(BF).reshape(ctx, OWN, hd)
    push("ctx", c, ctx, lambda peer: wg_to.at[peer], wg_from.at[c], send_sem.at[WG], recv_sem.at[WG])
    wg_from[c] = wg_to[c]

    kvg_stage[:, :hd] = key_grad
    kvg_stage[:, hd:] = kv_wide[1].astype(BF)
    outs = [pltpu.make_async_copy(kvg_stage, kvg_out, out_sem.at[0])]
    outs[0].start()

    drain(dq_from, roll, recv_sem.at[DQ])
    dq_all[r] = (jnp.sum(dq_from[...].astype(F32), axis=0) * scale).astype(BF)
    push(
        "roll", r, roll, lambda peer: dq_all.at[r], dq_all.at[r], send_sem.at[DQALL], recv_sem.at[DQALL]
    )

    for i in (7, 8, 9):
        loads[i].wait()
    drain(wg_from, ctx, recv_sem.at[WG])
    grad = jnp.sum(wg_from[...].astype(F32), axis=0)
    master = mw_in[...]
    new_first = BETA_ONE * m1_in[...] + (1.0 - BETA_ONE) * grad
    new_second = BETA_TWO * m2_in[...] + (1.0 - BETA_TWO) * grad * grad
    update = (
        new_first / CORRECT_ONE / (jnp.sqrt(new_second / CORRECT_TWO) + ADAM_EPS)
        + DECAY_RATE * master
    )
    new_master = master - LEARN_RATE * update
    rolled[r] = new_master.astype(BF)
    push("roll", r, roll, lambda peer: rolled.at[r], rolled.at[r], send_sem.at[ROLL], recv_sem.at[ROLL])
    mw_stage[...] = new_master
    m1_stage[...] = new_first
    m2_stage[...] = new_second
    for stage, out in ((mw_stage, mw_out), (m1_stage, m1_out), (m2_stage, m2_out)):
        outs.append(pltpu.make_async_copy(stage, out, out_sem.at[len(outs)]))
        outs[-1].start()

    drain(dq_all, roll, recv_sem.at[DQALL])
    flat = dq_all[...].reshape(HEADS * rows, hd)
    for h in range(HEADS):
        qg_stage[:, pl.ds(h * hd, hd)] = flat[h * rows : (h + 1) * rows]
    outs.append(pltpu.make_async_copy(qg_stage, qg_out, out_sem.at[len(outs)]))
    outs[-1].start()
    drain(rolled, roll, recv_sem.at[ROLL])
    outs.append(pltpu.make_async_copy(rolled, rw_out, out_sem.at[len(outs)]))
    outs[-1].start()

    for buf, count, which in (
        (kv, ctx, KV),
        (stats, roll, STATS),
        (dkv_to, ctx, DKV),
        (dq_to, roll, DQ),
        (dq_all, roll, DQALL),
        (kvg, roll, KVG),
        (wg_to, ctx, WG),
        (rolled, roll, ROLL),
    ):
        drain(buf, count, send_sem.at[which])
    for out in outs:
        out.wait()


def body(order, segments, layer_input, query, key, value, out_grad, master, first, second):
    ctx = lax.axis_size("ctx")
    roll = lax.axis_size("roll")
    rows, hd = key.shape
    width = query.shape[1]
    keys = ctx * SHARE
    piece = HEADS * SHARE
    shape = jax.ShapeDtypeStruct
    vmem = pltpu.VMEM
    anywhere = pl.BlockSpec(memory_space=pl.ANY)
    query_grad, key_value, new_master, new_first, new_second, rolled = pl.pallas_call(
        functools.partial(kernel, ctx, roll),
        out_shape=(
            shape((rows, width), BF),
            shape((rows, 2 * hd), BF),
            shape((OWN, hd), F32),
            shape((OWN, hd), F32),
            shape((OWN, hd), F32),
            shape((roll, OWN, hd), BF),
        ),
        in_specs=[pl.BlockSpec(memory_space=pltpu.HBM)] * 10,
        out_specs=[anywhere] * 6,
        scratch_shapes=[
            pltpu.SMEM((ctx,), jnp.int32),
            vmem((ctx, rows), jnp.int32),
            vmem((ctx, OWN, rows), BF),
            vmem((rows, width), BF),
            vmem((rows, hd), BF),
            vmem((rows, hd), BF),
            vmem((rows, width), BF),
            vmem((OWN, hd), F32),
            vmem((OWN, hd), F32),
            vmem((OWN, hd), F32),
            vmem((2, rows, hd), F32),
            vmem((keys, rows), F32),
            vmem((HEADS, keys, rows), F32),
            vmem((HEADS, keys, rows), F32),
            vmem((ctx, 2 * SHARE, hd), BF),
            vmem((roll, 3, 8, rows), F32),
            vmem((ctx, 2 * SHARE, hd), BF),
            vmem((ctx, 2 * SHARE, hd), BF),
            vmem((roll, piece, hd), BF),
            vmem((roll, piece, hd), BF),
            vmem((roll, piece, hd), BF),
            vmem((roll, 2 * SHARE, hd), BF),
            vmem((ctx, OWN, hd), BF),
            vmem((ctx, OWN, hd), BF),
            vmem((roll, OWN, hd), BF),
            vmem((rows, width), BF),
            vmem((rows, 2 * hd), BF),
            vmem((OWN, hd), F32),
            vmem((OWN, hd), F32),
            vmem((OWN, hd), F32),
            pltpu.SemaphoreType.DMA((10,)),
            pltpu.SemaphoreType.DMA((10,)),
            pltpu.SemaphoreType.DMA((10,)),
            pltpu.SemaphoreType.DMA((6,)),
        ],
        compiler_params=pltpu.CompilerParams(
            collective_id=0, has_side_effects=True, vmem_limit_bytes=56 * 1024 * 1024
        ),
    )(
        order,
        segments.reshape(ctx, rows),
        layer_input.reshape(ctx, roll, OWN, rows),
        query,
        key,
        value,
        out_grad,
        master,
        first,
        second,
    )
    return (
        query_grad,
        key_value,
        new_master,
        new_first,
        new_second,
        rolled.reshape(roll * OWN, hd),
    )


def solution(mesh):
    placed = (
        P(),
        P(),
        P(None, "ctx"),
        P("ctx", None),
        P("ctx", None),
        P("ctx", None),
        P("ctx", None),
        P(("ctx", "roll"), None),
        P(("ctx", "roll"), None),
        P(("ctx", "roll"), None),
    )
    return jax.shard_map(
        body,
        mesh=mesh,
        in_specs=placed,
        out_specs=(
            P("ctx", None),
            P("ctx", None),
            P(("ctx", "roll"), None),
            P(("ctx", "roll"), None),
            P(("ctx", "roll"), None),
            P("ctx", None),
        ),
        check_vma=False,
    )
```

```python
import functools

import jax
import jax.numpy as jnp
from jax import lax
from jax.experimental import pallas as pl
from jax.experimental.pallas import tpu as pltpu
from jax.sharding import PartitionSpec as P

NEG_FILL = -1e30
BETA_ONE = 0.9
BETA_TWO = 0.95
ADAM_EPS = 1e-08
DECAY_RATE = 0.1
LEARN_RATE = 1e-06
CORRECT_ONE = 0.9999734386011124
CORRECT_TWO = 0.994079470779666

MESH = pl.DeviceIdType.MESH
RING = 8
RUN = 4
SHARE = 8
OWN = 16
HEADS = 6
BF = jnp.bfloat16
F32 = jnp.float32

(KV, STATE, STATS, DKV, DQ, DQALL, KVG, WG, ROLL, BACK) = range(10)


class Place:
    def __init__(self, ctx, roll):
        self.zs, self.xs = ctx // RUN, roll // (2 * (RING // RUN))
        self.c, self.r = lax.axis_index("ctx"), lax.axis_index("roll")
        self.z = lax.rem(self.c, self.zs)
        self.x = lax.div(self.r, 4)
        self.core = lax.rem(self.r, 2)
        self.y = lax.div(self.c, self.zs) + RUN * lax.rem(lax.div(self.r, 2), 2)

    def turn(self, dy):
        return lax.rem(self.y + (dy + RING), RING)

    def block(self, y, z):
        return lax.rem(y, RUN) * self.zs + z

    def part(self, y, x=None, core=None):
        x = self.x if x is None else x
        core = self.core if core is None else core
        return x * 4 + lax.div(y, RUN) * 2 + core

    def device(self, y, z, x=None, core=None):
        return {"ctx": self.block(y, z), "roll": self.part(y, x, core)}

    def around_z(self, dz):
        return lax.rem(self.z + dz, self.zs)

    def across(self, steps):
        ways = [(dy, dx, dk) for dy in steps for dx in range(self.xs) for dk in range(2)]
        ways.sort(key=lambda w: -(min(w[0] % RING, -w[0] % RING) + min(w[1], self.xs - w[1])))
        return [
            (way, self.turn(way[0]), lax.rem(self.x + way[1], self.xs), lax.rem(self.core + way[2], 2))
            for way in ways
        ]

    def window(self, steps):
        ways = [(dy, dz) for dy in steps for dz in range(self.zs)]
        return sorted(ways, key=lambda w: -(abs(w[0]) + min(w[1], self.zs - w[1])))


def send(src, dst, sems, which, device):
    pltpu.make_async_remote_copy(
        src_ref=src,
        dst_ref=dst,
        send_sem=sems[0].at[which],
        recv_sem=sems[1].at[which],
        device_id=device,
        device_id_type=MESH,
    ).start()


def drain(part, sem):
    pltpu.make_async_copy(part, part, sem).wait()


def contract(left, right, dims):
    return lax.dot_general(left, right, (dims, ((), ())), preferred_element_type=F32)


def kernel(
    ctx,
    roll,
    order_hbm,
    seg_hbm,
    x_hbm,
    q_hbm,
    k_hbm,
    v_hbm,
    do_hbm,
    mw_hbm,
    m1_hbm,
    m2_hbm,
    qg_out,
    kvg_out,
    mw_out,
    m1_out,
    m2_out,
    rw_out,
    order,
    seg,
    x_in,
    q_in,
    k_in,
    v_in,
    do_in,
    state_in,
    state,
    state_new,
    state_back,
    kv_wide,
    bias,
    expo,
    dprob,
    kv,
    kv_other,
    stats,
    dkv_to,
    dkv_from,
    dq_to,
    dq_from,
    dq_all,
    kvg,
    kvg_own,
    wg_to,
    wg_from,
    rolled,
    rolled_own,
    kvg_stage,
    load_sem,
    send_sem,
    recv_sem,
    out_sem,
):
    at = Place(ctx, roll)
    c, r = at.c, at.r
    sems = (send_sem, recv_sem)
    rows = k_in.shape[0]
    hd = k_in.shape[1]
    keys = ctx * SHARE
    scale = hd**-0.5
    piece = HEADS * SHARE
    zs = at.zs
    most = pl.ds(0, ctx - 1)
    others = pl.ds(0, roll - 1)

    class_home = [
        lax.rem(at.y + RING - lax.rem(at.y + RING - j, RUN), RING) for j in range(RUN)
    ]
    class_part = [at.part(home) for home in class_home]

    pairs = [(k_hbm, k_in), (v_hbm, v_in), (order_hbm, order), (seg_hbm, seg)]
    pairs += [(src, state_in.at[i]) for i, src in enumerate((mw_hbm, m1_hbm, m2_hbm))]
    pairs += [(q_hbm, q_in), (do_hbm, do_in)]
    pairs += [
        (x_hbm.at[pl.ds(j * zs, zs), class_part[j]], x_in.at[pl.ds(j * zs, zs)]) for j in range(RUN)
    ]
    loads = [
        pltpu.make_async_copy(src, dst, load_sem.at[i]) for i, (src, dst) in enumerate(pairs)
    ]
    for load in loads:
        load.start()

    barrier = pltpu.get_barrier_semaphore()
    greeted = 0

    def greet(device):
        pl.semaphore_signal(barrier, inc=1, device_id=device, device_id_type=MESH)

    for dy, dz in at.window((1, 0, -1, -2)):
        if (dy, dz) != (0, 0):
            greet(at.device(at.turn(dy), at.around_z(dz)))
            greeted += 1
    for way, y, x, core in at.across((2, -2, 0, 4)):
        if way not in ((0, 0, 0), (-2, 0, 0)):
            greet(at.device(y, at.z, x, core))
            greeted += 1

    loads[0].wait()
    loads[1].wait()
    kv_wide[0] = k_in[...].astype(F32)
    kv_wide[1] = v_in[...].astype(F32)

    def chunk(part):
        first = pl.multiple_of(part * SHARE, SHARE)
        both = [kv_wide[i, pl.ds(first, SHARE), :] for i in range(2)]
        return jnp.concatenate(both, axis=0).astype(BF)

    kv[c] = chunk(r)
    kv_other[...] = chunk(at.part(at.turn(4)))
    pl.semaphore_wait(barrier, greeted)
    for dy, dz in at.window((2, 1, 0, -1)):
        if (dy, dz) != (0, 0):
            src = kv_other if dy == -1 else kv.at[c]
            send(src, kv.at[c], sems, KV, at.device(at.turn(dy), at.around_z(dz)))
    for i in (4, 5, 6):
        loads[i].wait()
    send(state_in, state, sems, STATE, at.device(at.turn(2), at.z))

    loads[2].wait()
    loads[3].wait()
    ids = seg[...]
    q_seg = seg[pl.ds(c, 1), :]
    lane = lax.broadcasted_iota(jnp.int32, (1, rows), 1)
    q_pos = order[c] * rows + lane
    start = jnp.zeros((1, rows), F32)
    for rollout in range(3):
        total = jnp.sum(jnp.where(ids == rollout, 1.0, 0.0), axis=0, keepdims=True)
        total = jnp.sum(total, axis=1, keepdims=True)
        start = start + jnp.where(q_seg > rollout, total, 0.0)
    start = start.astype(jnp.int32)
    sub = lax.broadcasted_iota(jnp.int32, (SHARE, rows), 0)
    latest = q_pos - sub
    earliest = start - sub
    for block in range(ctx):
        base = order[block] * rows + class_part[block // zs] * SHARE
        seen = (latest >= base) & (earliest <= base)
        bias[pl.ds(block * SHARE, SHARE), :] = jnp.where(seen, 0.0, NEG_FILL)

    loads[7].wait()
    loads[8].wait()
    heads = [pl.ds(h * hd, hd) for h in range(HEADS)]
    lanes = [pl.ds(h * rows, rows) for h in range(HEADS)]
    q_rows = jnp.concatenate([q_in[:, cols] for cols in heads], axis=0)
    do_rows = jnp.concatenate([do_in[:, cols] for cols in heads], axis=0)
    drain(kv.at[most], recv_sem.at[KV])
    wide = kv[...].astype(F32)
    key = wide[:, :SHARE, :].reshape(keys, hd).astype(BF)
    value = wide[:, SHARE:, :].reshape(keys, hd).astype(BF)
    expo[...] = contract(key, q_rows, ((1,), (1,)))
    dprob[...] = contract(value, do_rows, ((1,), (1,)))
    for h in range(HEADS):
        scores = expo[:, lanes[h]] * scale + bias[...]
        top = jnp.max(scores, axis=0, keepdims=True)
        weights = jnp.exp(scores - top)
        expo[:, lanes[h]] = weights
        stats[r, 0, h : h + 1] = top
        stats[r, 1, h : h + 1] = jnp.sum(weights, axis=0, keepdims=True)
        stats[r, 2, h : h + 1] = jnp.sum(weights * dprob[:, lanes[h]], axis=0, keepdims=True)
    for i in range(3):
        stats[r, i, HEADS:] = jnp.zeros((8 - HEADS, rows), F32)
    for way, y, x, core in at.across((4, 0)):
        if way != (0, 0, 0):
            send(stats.at[r], stats.at[r], sems, STATS, at.device(y, at.z, x, core))
    own_top = stats[r, 0]
    drain(stats.at[others], recv_sem.at[STATS])
    top = jnp.max(stats[:, 0], axis=0)
    factor = jnp.exp(stats[:, 0] - top[None])
    total = jnp.sum(stats[:, 1] * factor, axis=0)
    delta = jnp.sum(stats[:, 2] * factor, axis=0) / total
    norm = jnp.exp(own_top - top) / total

    probs, dscores = [], []
    for h in range(HEADS):
        prob = expo[:, lanes[h]] * norm[h : h + 1]
        dscores.append((prob * (dprob[:, lanes[h]] - delta[h : h + 1])).astype(BF))
        probs.append(prob.astype(BF))
    dscore = jnp.concatenate(dscores, axis=1)
    key_grad = contract(dscore, q_rows, ((1,), (0,))) * scale
    value_grad = contract(jnp.concatenate(probs, axis=1), do_rows, ((1,), (0,)))
    both = jnp.concatenate(
        [key_grad.reshape(ctx, SHARE, hd), value_grad.reshape(ctx, SHARE, hd)], axis=1
    )
    dkv_to[...] = both.astype(BF)

    back = at.turn(-2)
    back_block = at.block(back, at.z)
    back_part = at.part(back)

    def scatter(to, arrived, which):
        for dy, dz in at.window((2, 1, 0, -1)):
            z = at.around_z(dz)
            if (dy, dz) != (0, 0):
                home = at.block(at.turn(dy - 2), z)
                send(to.at[home], arrived.at[c], sems, which, at.device(at.turn(dy), z))
        arrived[c] = to[back_block]

    scatter(dkv_to, dkv_from, DKV)

    dq_to[...] = contract(dscore, key, ((0,), (0,))).astype(BF)

    def dq_piece(part):
        return pl.ds(pl.multiple_of(part * piece, 16), piece)

    for way, y, x, core in at.across((4, 0)):
        if way != (0, 0, 0):
            src = dq_to.at[dq_piece(at.part(y, x, core))]
            send(src, dq_from.at[r], sems, DQ, at.device(y, at.z, x, core))
    dq_from[r] = dq_to[dq_piece(r)]

    drain(dkv_from.at[most], recv_sem.at[DKV])
    kvg_own[...] = jnp.sum(dkv_from[...].astype(F32), axis=0).astype(BF)

    def spread(own, arrived, which):
        for _, y, x, core in at.across((2, -2)):
            send(own, arrived.at[back_part], sems, which, at.device(y, at.z, x, core))

    spread(kvg_own, kvg, KVG)
    for load in loads[9:]:
        load.wait()
    drain(kvg, recv_sem.at[KVG])
    wide = kvg[...].astype(F32)
    kv_wide[0] = wide[:, :SHARE, :].reshape(rows, hd)
    kv_wide[1] = wide[:, SHARE:, :].reshape(rows, hd)
    key_grad = kv_wide[0].astype(BF)
    product = contract(x_in[...].reshape(ctx * OWN, rows), key_grad, ((1,), (0,)))
    wg_to[...] = product.astype(BF).reshape(ctx, OWN, hd)
    scatter(wg_to, wg_from, WG)

    kvg_stage[:, :hd] = key_grad
    kvg_stage[:, hd:] = kv_wide[1].astype(BF)
    outs = []

    def put(src, dst):
        outs.append(pltpu.make_async_copy(src, dst, out_sem.at[len(outs)]))
        outs[-1].start()

    put(kvg_stage, kvg_out)
    drain(dq_from.at[others], recv_sem.at[DQ])
    dq_all[dq_piece(r)] = (jnp.sum(dq_from[...].astype(F32), axis=0) * scale).astype(BF)
    for way, y, x, core in at.across((4, 0)):
        if way != (0, 0, 0):
            mine = dq_all.at[dq_piece(r)]
            send(mine, mine, sems, DQALL, at.device(y, at.z, x, core))

    drain(state, recv_sem.at[STATE])
    drain(wg_from.at[most], recv_sem.at[WG])
    grad = jnp.sum(wg_from[...].astype(F32), axis=0)
    master = state[0]
    new_first = BETA_ONE * state[1] + (1.0 - BETA_ONE) * grad
    new_second = BETA_TWO * state[2] + (1.0 - BETA_TWO) * grad * grad
    update = (
        new_first / CORRECT_ONE / (jnp.sqrt(new_second / CORRECT_TWO) + ADAM_EPS)
        + DECAY_RATE * master
    )
    new_master = master - LEARN_RATE * update
    rolled_own[...] = new_master.astype(BF)
    spread(rolled_own, rolled, ROLL)
    state_new[0] = new_master
    state_new[1] = new_first
    state_new[2] = new_second
    send(state_new, state_back, sems, BACK, at.device(back, at.z))

    dq_most = pl.ds(0, (roll - 1) * piece)
    drain(dq_all.at[dq_most], recv_sem.at[DQALL])
    for h in range(HEADS):
        put(dq_all.at[pl.ds(h * rows, rows)], qg_out.at[:, heads[h]])
    drain(kv.at[most], send_sem.at[KV])
    drain(state_in, send_sem.at[STATE])
    drain(stats.at[others], send_sem.at[STATS])
    drain(dkv_to.at[most], send_sem.at[DKV])
    drain(dq_to.at[dq_most], send_sem.at[DQ])
    drain(kvg, send_sem.at[KVG])
    drain(wg_to.at[most], send_sem.at[WG])
    drain(dq_all.at[dq_most], send_sem.at[DQALL])
    drain(state_back, recv_sem.at[BACK])
    for i, out in enumerate((mw_out, m1_out, m2_out)):
        put(state_back.at[i], out)
    drain(rolled, recv_sem.at[ROLL])
    put(rolled, rw_out)
    drain(rolled, send_sem.at[ROLL])
    drain(state_new, send_sem.at[BACK])
    for out in outs:
        out.wait()


def hand_over(*refs):
    *arrays, sem = refs
    half = len(arrays) // 2
    copies = [
        pltpu.make_async_copy(src, dst, sem.at[i])
        for i, (src, dst) in enumerate(zip(arrays[:half], arrays[half:]))
    ]
    for copy in copies:
        copy.start()
    for copy in copies:
        copy.wait()


def body(order, segments, layer_input, query, key, value, out_grad, master, first, second):
    ctx = lax.axis_size("ctx")
    roll = lax.axis_size("roll")
    rows, hd = key.shape
    width = query.shape[1]
    keys = ctx * SHARE
    piece = HEADS * SHARE
    shape = jax.ShapeDtypeStruct
    vmem = pltpu.VMEM
    anywhere = pl.BlockSpec(memory_space=pl.ANY)
    shapes = (
        shape((rows, width), BF),
        shape((rows, 2 * hd), BF),
        shape((OWN, hd), F32),
        shape((OWN, hd), F32),
        shape((OWN, hd), F32),
        shape((roll, OWN, hd), BF),
    )
    made = pl.pallas_call(
        functools.partial(kernel, ctx, roll),
        out_shape=shapes,
        in_specs=[anywhere] * 10,
        out_specs=[anywhere] * 6,
        scratch_shapes=[
            pltpu.SMEM((ctx,), jnp.int32),
            vmem((ctx, rows), jnp.int32),
            vmem((ctx, OWN, rows), BF),
            vmem((rows, width), BF),
            vmem((rows, hd), BF),
            vmem((rows, hd), BF),
            vmem((rows, width), BF),
            vmem((3, OWN, hd), F32),
            vmem((3, OWN, hd), F32),
            vmem((3, OWN, hd), F32),
            vmem((3, OWN, hd), F32),
            vmem((2, rows, hd), F32),
            vmem((keys, rows), F32),
            vmem((keys, HEADS * rows), F32),
            vmem((keys, HEADS * rows), F32),
            vmem((ctx, 2 * SHARE, hd), BF),
            vmem((2 * SHARE, hd), BF),
            vmem((roll, 3, 8, rows), F32),
            vmem((ctx, 2 * SHARE, hd), BF),
            vmem((ctx, 2 * SHARE, hd), BF),
            vmem((roll * piece, hd), BF),
            vmem((roll, piece, hd), BF),
            vmem((roll * piece, hd), BF),
            vmem((roll, 2 * SHARE, hd), BF),
            vmem((2 * SHARE, hd), BF),
            vmem((ctx, OWN, hd), BF),
            vmem((ctx, OWN, hd), BF),
            vmem((roll, OWN, hd), BF),
            vmem((OWN, hd), BF),
            vmem((rows, 2 * hd), BF),
            pltpu.SemaphoreType.DMA((13,)),
            pltpu.SemaphoreType.DMA((10,)),
            pltpu.SemaphoreType.DMA((10,)),
            pltpu.SemaphoreType.DMA((12,)),
        ],
        compiler_params=pltpu.CompilerParams(
            collective_id=0, has_side_effects=True, vmem_limit_bytes=56 * 1024 * 1024
        ),
    )(
        order,
        segments.reshape(ctx, rows),
        layer_input.reshape(ctx, roll, OWN, rows),
        query,
        key,
        value,
        out_grad,
        master,
        first,
        second,
    )
    query_grad, key_value, new_master, new_first, new_second, rolled = pl.pallas_call(
        hand_over,
        out_shape=shapes,
        in_specs=[anywhere] * 6,
        out_specs=[anywhere] * 6,
        scratch_shapes=[pltpu.SemaphoreType.DMA((6,))],
    )(*made)
    return (
        query_grad,
        key_value,
        new_master,
        new_first,
        new_second,
        rolled.reshape(roll * OWN, hd),
    )


def solution(mesh):
    placed = (
        P(),
        P(),
        P(None, "ctx"),
        P("ctx", None),
        P("ctx", None),
        P("ctx", None),
        P("ctx", None),
        P(("ctx", "roll"), None),
        P(("ctx", "roll"), None),
        P(("ctx", "roll"), None),
    )
    return jax.shard_map(
        body,
        mesh=mesh,
        in_specs=placed,
        out_specs=(
            P("ctx", None),
            P("ctx", None),
            P(("ctx", "roll"), None),
            P(("ctx", "roll"), None),
            P(("ctx", "roll"), None),
            P("ctx", None),
        ),
        check_vma=False,
    )
```

```python
import functools

import jax
import jax.numpy as jnp
from jax import lax
from jax.experimental import pallas as pl
from jax.experimental.pallas import tpu as pltpu
from jax.sharding import PartitionSpec as P

NEG_FILL = -1e30
BETA_ONE = 0.9
BETA_TWO = 0.95
ADAM_EPS = 1e-08
DECAY_RATE = 0.1
LEARN_RATE = 1e-06
CORRECT_ONE = 0.9999734386011124
CORRECT_TWO = 0.994079470779666

MESH = pl.DeviceIdType.MESH
RING = 8
RUN = 4
SHARE = 8
OWN = 16
HEADS = 6
BF = jnp.bfloat16
F32 = jnp.float32

(KV, STATE, STATS, DKV, DQ, DQALL, KVG, WG, ROLL, BACK) = range(10)


class Place:
    def __init__(self, ctx, roll):
        self.zs, self.xs = ctx // RUN, roll // (2 * (RING // RUN))
        self.c, self.r = lax.axis_index("ctx"), lax.axis_index("roll")
        self.z = lax.rem(self.c, self.zs)
        self.x = lax.div(self.r, 4)
        self.core = lax.rem(self.r, 2)
        self.y = lax.div(self.c, self.zs) + RUN * lax.rem(lax.div(self.r, 2), 2)

    def turn(self, dy):
        return lax.rem(self.y + (dy + RING), RING)

    def block(self, y, z):
        return lax.rem(y, RUN) * self.zs + z

    def part(self, y, x=None, core=None):
        x = self.x if x is None else x
        core = self.core if core is None else core
        return x * 4 + lax.div(y, RUN) * 2 + core

    def device(self, y, z, x=None, core=None):
        return {"ctx": self.block(y, z), "roll": self.part(y, x, core)}

    def around_z(self, dz):
        return lax.rem(self.z + dz, self.zs)

    def across(self, steps):
        ways = [(dy, dx, dk) for dy in steps for dx in range(self.xs) for dk in range(2)]
        ways.sort(key=lambda w: -(min(w[0] % RING, -w[0] % RING) + min(w[1], self.xs - w[1])))
        return [
            (way, self.turn(way[0]), lax.rem(self.x + way[1], self.xs), lax.rem(self.core + way[2], 2))
            for way in ways
        ]

    def window(self, steps):
        ways = [(dy, dz) for dy in steps for dz in range(self.zs)]
        return sorted(ways, key=lambda w: -(abs(w[0]) + min(w[1], self.zs - w[1])))


def send(src, dst, sems, which, device):
    pltpu.make_async_remote_copy(
        src_ref=src,
        dst_ref=dst,
        send_sem=sems[0].at[which],
        recv_sem=sems[1].at[which],
        device_id=device,
        device_id_type=MESH,
    ).start()


def drain(part, sem):
    pltpu.make_async_copy(part, part, sem).wait()


def contract(left, right, dims):
    return lax.dot_general(left, right, (dims, ((), ())), preferred_element_type=F32)


def kernel(
    ctx,
    roll,
    order_hbm,
    seg_hbm,
    x_hbm,
    q_hbm,
    k_hbm,
    v_hbm,
    do_hbm,
    mw_hbm,
    m1_hbm,
    m2_hbm,
    qg_out,
    kvg_out,
    mw_out,
    m1_out,
    m2_out,
    rw_out,
    order,
    seg,
    x_in,
    q_in,
    k_in,
    v_in,
    do_in,
    state_in,
    state,
    state_new,
    kv_wide,
    bias,
    expo,
    dprob,
    kv,
    kv_other,
    tops,
    stats,
    dkv_to,
    dkv_from,
    dq_to,
    dq_from,
    dq_own,
    kvg,
    kvg_own,
    wg_to,
    wg_from,
    rolled_own,
    kvg_stage,
    load_sem,
    send_sem,
    recv_sem,
    out_sem,
):
    at = Place(ctx, roll)
    c, r = at.c, at.r
    sems = (send_sem, recv_sem)
    rows = k_in.shape[0]
    hd = k_in.shape[1]
    keys = ctx * SHARE
    scale = hd**-0.5
    piece = HEADS * SHARE
    zs = at.zs
    most = pl.ds(0, ctx - 1)
    others = pl.ds(0, roll - 1)

    class_home = [
        lax.rem(at.y + RING - lax.rem(at.y + RING - j, RUN), RING) for j in range(RUN)
    ]
    class_part = [at.part(home) for home in class_home]

    pairs = [(k_hbm, k_in), (v_hbm, v_in), (order_hbm, order), (seg_hbm, seg)]
    pairs += [(src, state_in.at[i]) for i, src in enumerate((mw_hbm, m1_hbm, m2_hbm))]
    pairs += [(q_hbm, q_in), (do_hbm, do_in)]
    pairs += [
        (x_hbm.at[pl.ds(j * zs, zs), class_part[j]], x_in.at[pl.ds(j * zs, zs)]) for j in range(RUN)
    ]
    loads = [
        pltpu.make_async_copy(src, dst, load_sem.at[i]) for i, (src, dst) in enumerate(pairs)
    ]
    for load in loads[:2]:
        load.start()

    barrier = pltpu.get_barrier_semaphore()
    greeted = 0

    def greet(device):
        pl.semaphore_signal(barrier, inc=1, device_id=device, device_id_type=MESH)

    for dy, dz in at.window((1, 0, -1, -2)):
        if (dy, dz) != (0, 0):
            greet(at.device(at.turn(dy), at.around_z(dz)))
            greeted += 1
    for way, y, x, core in at.across((2, -2, 0, 4)):
        if way not in ((0, 0, 0), (-2, 0, 0)):
            greet(at.device(y, at.z, x, core))
            greeted += 1

    for load in loads[2:]:
        load.start()

    loads[0].wait()
    loads[1].wait()
    kv_wide[0] = k_in[...].astype(F32)
    kv_wide[1] = v_in[...].astype(F32)

    def chunk(part):
        first = pl.multiple_of(part * SHARE, SHARE)
        both = [kv_wide[i, pl.ds(first, SHARE), :] for i in range(2)]
        return jnp.concatenate(both, axis=0).astype(BF)

    kv[c] = chunk(r)
    kv_other[...] = chunk(at.part(at.turn(4)))
    pl.semaphore_wait(barrier, greeted)
    for dy, dz in at.window((2, 1, 0, -1)):
        if (dy, dz) != (0, 0):
            src = kv_other if dy == -1 else kv.at[c]
            send(src, kv.at[c], sems, KV, at.device(at.turn(dy), at.around_z(dz)))
    for i in (4, 5, 6):
        loads[i].wait()
    send(state_in, state, sems, STATE, at.device(at.turn(2), at.z))

    loads[2].wait()
    loads[3].wait()
    ids = seg[...]
    q_seg = seg[pl.ds(c, 1), :]
    lane = lax.broadcasted_iota(jnp.int32, (1, rows), 1)
    q_pos = order[c] * rows + lane
    start = jnp.zeros((1, rows), F32)
    for rollout in range(3):
        total = jnp.sum(jnp.where(ids == rollout, 1.0, 0.0), axis=0, keepdims=True)
        total = jnp.sum(total, axis=1, keepdims=True)
        start = start + jnp.where(q_seg > rollout, total, 0.0)
    start = start.astype(jnp.int32)
    sub = lax.broadcasted_iota(jnp.int32, (SHARE, rows), 0)
    latest = q_pos - sub
    earliest = start - sub
    for block in range(ctx):
        base = order[block] * rows + class_part[block // zs] * SHARE
        seen = (latest >= base) & (earliest <= base)
        bias[pl.ds(block * SHARE, SHARE), :] = jnp.where(seen, 0.0, NEG_FILL)

    loads[7].wait()
    loads[8].wait()
    heads = [pl.ds(h * hd, hd) for h in range(HEADS)]
    lanes = [pl.ds(h * rows, rows) for h in range(HEADS)]
    q_rows = jnp.concatenate([q_in[:, cols] for cols in heads], axis=0)
    do_rows = jnp.concatenate([do_in[:, cols] for cols in heads], axis=0)
    drain(kv.at[most], recv_sem.at[KV])
    wide = kv[...].astype(F32)
    key = wide[:, :SHARE, :].reshape(keys, hd).astype(BF)
    value = wide[:, SHARE:, :].reshape(keys, hd).astype(BF)
    expo[...] = contract(key, q_rows, ((1,), (1,)))
    dprob[...] = contract(value, do_rows, ((1,), (1,)))
    for h in range(HEADS):
        scores = expo[:, lanes[h]] * scale + bias[...]
        top = jnp.max(scores, axis=0, keepdims=True)
        weights = jnp.exp(scores - top)
        expo[:, lanes[h]] = weights
        total = jnp.sum(weights, axis=0, keepdims=True)
        tops[h : h + 1] = top
        stats[r, 0, h : h + 1] = top + jnp.log(total)
        stats[r, 1, h : h + 1] = (
            jnp.sum(weights * dprob[:, lanes[h]], axis=0, keepdims=True) / total
        )
    tops[HEADS:] = jnp.zeros((8 - HEADS, rows), F32)
    for i in range(2):
        stats[r, i, HEADS:] = jnp.zeros((8 - HEADS, rows), F32)
    for way, y, x, core in at.across((4, 0)):
        if way != (0, 0, 0):
            send(stats.at[r], stats.at[r], sems, STATS, at.device(y, at.z, x, core))
    drain(stats.at[others], recv_sem.at[STATS])
    top = jnp.max(stats[:, 0], axis=0)
    factor = jnp.exp(stats[:, 0] - top[None])
    total = jnp.sum(factor, axis=0)
    delta = jnp.sum(stats[:, 1] * factor, axis=0) / total
    norm = jnp.exp(tops[...] - top) / total

    probs, dscores = [], []
    for h in range(HEADS):
        prob = expo[:, lanes[h]] * norm[h : h + 1]
        dscores.append((prob * (dprob[:, lanes[h]] - delta[h : h + 1])).astype(BF))
        probs.append(prob.astype(BF))
    dscore = jnp.concatenate(dscores, axis=1)
    key_grad = contract(dscore, q_rows, ((1,), (0,))) * scale
    value_grad = contract(jnp.concatenate(probs, axis=1), do_rows, ((1,), (0,)))
    both = jnp.concatenate(
        [key_grad.reshape(ctx, SHARE, hd), value_grad.reshape(ctx, SHARE, hd)], axis=1
    )
    dkv_to[...] = both.astype(BF)

    back = at.turn(-2)
    back_block = at.block(back, at.z)
    back_part = at.part(back)

    def scatter(to, arrived, which):
        for dy, dz in at.window((2, 1, 0, -1)):
            z = at.around_z(dz)
            if (dy, dz) != (0, 0):
                home = at.block(at.turn(dy - 2), z)
                send(to.at[home], arrived.at[c], sems, which, at.device(at.turn(dy), z))
        arrived[c] = to[back_block]

    scatter(dkv_to, dkv_from, DKV)

    drain(dkv_from.at[most], recv_sem.at[DKV])
    kvg_own[...] = jnp.sum(dkv_from[...].astype(F32), axis=0).astype(BF)

    def spread(own, arrived, which):
        for _, y, x, core in at.across((2, -2)):
            send(own, arrived.at[back_part], sems, which, at.device(y, at.z, x, core))

    spread(kvg_own, kvg, KVG)

    dq_to[...] = contract(dscore, key, ((0,), (0,))).astype(BF)

    def dq_piece(part):
        return pl.ds(pl.multiple_of(part * piece, 16), piece)

    for way, y, x, core in at.across((4, 0)):
        if way != (0, 0, 0):
            src = dq_to.at[dq_piece(at.part(y, x, core))]
            send(src, dq_from.at[r], sems, DQ, at.device(y, at.z, x, core))
    dq_from[r] = dq_to[dq_piece(r)]
    for load in loads[9:]:
        load.wait()
    drain(kvg, recv_sem.at[KVG])
    wide = kvg[...].astype(F32)
    kv_wide[0] = wide[:, :SHARE, :].reshape(rows, hd)
    kv_wide[1] = wide[:, SHARE:, :].reshape(rows, hd)
    key_grad = kv_wide[0].astype(BF)
    product = contract(x_in[...].reshape(ctx * OWN, rows), key_grad, ((1,), (0,)))
    wg_to[...] = product.astype(BF).reshape(ctx, OWN, hd)
    scatter(wg_to, wg_from, WG)

    kvg_stage[:, :hd] = key_grad
    kvg_stage[:, hd:] = kv_wide[1].astype(BF)
    outs = []

    def put(src, dst):
        outs.append(pltpu.make_async_copy(src, dst, out_sem.at[len(outs)]))
        outs[-1].start()

    put(kvg_stage, kvg_out)
    drain(dq_from.at[others], recv_sem.at[DQ])
    dq_own[...] = (jnp.sum(dq_from[...].astype(F32), axis=0) * scale).astype(BF)
    mine = qg_out.at[dq_piece(r)]
    for way, y, x, core in at.across((4, 0)):
        if way != (0, 0, 0):
            send(dq_own, mine, sems, DQALL, at.device(y, at.z, x, core))
    put(dq_own, mine)

    drain(state, recv_sem.at[STATE])
    drain(wg_from.at[most], recv_sem.at[WG])
    grad = jnp.sum(wg_from[...].astype(F32), axis=0)
    master = state[0]
    new_first = BETA_ONE * state[1] + (1.0 - BETA_ONE) * grad
    new_second = BETA_TWO * state[2] + (1.0 - BETA_TWO) * grad * grad
    update = (
        new_first / CORRECT_ONE / (jnp.sqrt(new_second / CORRECT_TWO) + ADAM_EPS)
        + DECAY_RATE * master
    )
    new_master = master - LEARN_RATE * update
    rolled_own[...] = new_master.astype(BF)
    spread(rolled_own, rw_out, ROLL)
    state_new[0] = new_master
    state_new[1] = new_first
    state_new[2] = new_second
    for i, out in enumerate((mw_out, m1_out, m2_out)):
        send(state_new.at[i], out, sems, BACK, at.device(back, at.z))

    dq_most = pl.ds(0, (roll - 1) * piece)
    drain(kv.at[most], send_sem.at[KV])
    drain(state_in, send_sem.at[STATE])
    drain(stats.at[others], send_sem.at[STATS])
    drain(dkv_to.at[most], send_sem.at[DKV])
    drain(dq_to.at[dq_most], send_sem.at[DQ])
    drain(kvg, send_sem.at[KVG])
    drain(wg_to.at[most], send_sem.at[WG])
    drain(dq_to.at[dq_most], send_sem.at[DQALL])
    drain(kvg, send_sem.at[ROLL])
    drain(state_new, send_sem.at[BACK])
    drain(state_new, recv_sem.at[BACK])
    drain(dq_to.at[dq_most], recv_sem.at[DQALL])
    drain(kvg, recv_sem.at[ROLL])
    for out in outs:
        out.wait()


def hand_over(*refs):
    sources, places, held, sem = refs[:6], refs[6:12], refs[12:18], refs[18]
    rows, hd = places[0].shape[0], sources[0].shape[1]
    pairs = [(i, src, held[i]) for i, src in enumerate(sources)][1:]
    pairs += [
        (0, sources[0].at[pl.ds(h * rows, rows)], held[0].at[:, pl.ds(h * hd, hd)])
        for h in range(HEADS)
    ]
    fetches = [
        (i, pltpu.make_async_copy(src, dst, sem.at[0, n])) for n, (i, src, dst) in enumerate(pairs)
    ]
    writes = [
        pltpu.make_async_copy(src, dst, sem.at[1, i])
        for i, (src, dst) in enumerate(zip(held, places))
    ]
    for _, fetch in fetches:
        fetch.start()
    for i, fetch in fetches:
        fetch.wait()
        if i > 0:
            writes[i].start()
    writes[0].start()
    for write in writes:
        write.wait()


def body(order, segments, layer_input, query, key, value, out_grad, master, first, second):
    ctx = lax.axis_size("ctx")
    roll = lax.axis_size("roll")
    rows, hd = key.shape
    width = query.shape[1]
    keys = ctx * SHARE
    piece = HEADS * SHARE
    shape = jax.ShapeDtypeStruct
    vmem = pltpu.VMEM
    anywhere = pl.BlockSpec(memory_space=pl.ANY)
    shapes = (
        shape((rows, width), BF),
        shape((rows, 2 * hd), BF),
        shape((OWN, hd), F32),
        shape((OWN, hd), F32),
        shape((OWN, hd), F32),
        shape((roll, OWN, hd), BF),
    )
    made = pl.pallas_call(
        functools.partial(kernel, ctx, roll),
        out_shape=(shape((HEADS * rows, hd), BF), *shapes[1:]),
        in_specs=[anywhere] * 10,
        out_specs=[anywhere] * 6,
        scratch_shapes=[
            pltpu.SMEM((ctx,), jnp.int32),
            vmem((ctx, rows), jnp.int32),
            vmem((ctx, OWN, rows), BF),
            vmem((rows, width), BF),
            vmem((rows, hd), BF),
            vmem((rows, hd), BF),
            vmem((rows, width), BF),
            vmem((3, OWN, hd), F32),
            vmem((3, OWN, hd), F32),
            vmem((3, OWN, hd), F32),
            vmem((2, rows, hd), F32),
            vmem((keys, rows), F32),
            vmem((keys, HEADS * rows), F32),
            vmem((keys, HEADS * rows), F32),
            vmem((ctx, 2 * SHARE, hd), BF),
            vmem((2 * SHARE, hd), BF),
            vmem((8, rows), F32),
            vmem((roll, 2, 8, rows), F32),
            vmem((ctx, 2 * SHARE, hd), BF),
            vmem((ctx, 2 * SHARE, hd), BF),
            vmem((roll * piece, hd), BF),
            vmem((roll, piece, hd), BF),
            vmem((piece, hd), BF),
            vmem((roll, 2 * SHARE, hd), BF),
            vmem((2 * SHARE, hd), BF),
            vmem((ctx, OWN, hd), BF),
            vmem((ctx, OWN, hd), BF),
            vmem((OWN, hd), BF),
            vmem((rows, 2 * hd), BF),
            pltpu.SemaphoreType.DMA((13,)),
            pltpu.SemaphoreType.DMA((10,)),
            pltpu.SemaphoreType.DMA((10,)),
            pltpu.SemaphoreType.DMA((12,)),
        ],
        compiler_params=pltpu.CompilerParams(
            collective_id=0, has_side_effects=True, vmem_limit_bytes=56 * 1024 * 1024
        ),
    )(
        order,
        segments.reshape(ctx, rows),
        layer_input.reshape(ctx, roll, OWN, rows),
        query,
        key,
        value,
        out_grad,
        master,
        first,
        second,
    )
    query_grad, key_value, new_master, new_first, new_second, rolled = pl.pallas_call(
        hand_over,
        out_shape=shapes,
        in_specs=[anywhere] * 6,
        out_specs=[anywhere] * 6,
        scratch_shapes=[*(vmem(s.shape, s.dtype) for s in shapes), pltpu.SemaphoreType.DMA((2, 11))],
    )(*made)
    return (
        query_grad,
        key_value,
        new_master,
        new_first,
        new_second,
        rolled.reshape(roll * OWN, hd),
    )


def solution(mesh):
    placed = (
        P(),
        P(),
        P(None, "ctx"),
        P("ctx", None),
        P("ctx", None),
        P("ctx", None),
        P("ctx", None),
        P(("ctx", "roll"), None),
        P(("ctx", "roll"), None),
        P(("ctx", "roll"), None),
    )
    return jax.shard_map(
        body,
        mesh=mesh,
        in_specs=placed,
        out_specs=(
            P("ctx", None),
            P("ctx", None),
            P(("ctx", "roll"), None),
            P(("ctx", "roll"), None),
            P(("ctx", "roll"), None),
            P("ctx", None),
        ),
        check_vma=False,
    )
```

```python
import functools

import jax
import jax.numpy as jnp
from jax import lax
from jax.experimental import pallas as pl
from jax.experimental.pallas import tpu as pltpu
from jax.sharding import PartitionSpec as P

NEG_FILL = -1e30
BETA_ONE = 0.9
BETA_TWO = 0.95
ADAM_EPS = 1e-08
DECAY_RATE = 0.1
LEARN_RATE = 1e-06
CORRECT_ONE = 0.9999734386011124
CORRECT_TWO = 0.994079470779666

MESH = pl.DeviceIdType.MESH
RING = 8
RUN = 4
SHARE = 8
OWN = 16
HEADS = 6
BF = jnp.bfloat16
F32 = jnp.float32

(KV, STATE, STATS, DKV, PAIR, DQ, DQALL, GIVE, KVG, WG, ROLL, BACK) = range(12)


class Place:
    def __init__(self, ctx, roll):
        self.zs, self.xs = ctx // RUN, roll // (2 * (RING // RUN))
        self.c, self.r = lax.axis_index("ctx"), lax.axis_index("roll")
        self.z = lax.rem(self.c, self.zs)
        self.x = lax.div(self.r, 4)
        self.core = lax.rem(self.r, 2)
        self.y = lax.div(self.c, self.zs) + RUN * lax.rem(lax.div(self.r, 2), 2)

    def turn(self, dy):
        return lax.rem(self.y + (dy + RING), RING)

    def block(self, y, z):
        return lax.rem(y, RUN) * self.zs + z

    def part(self, y, x=None, core=None):
        x = self.x if x is None else x
        core = self.core if core is None else core
        return x * 4 + lax.div(y, RUN) * 2 + core

    def device(self, y, z, x=None, core=None):
        return {"ctx": self.block(y, z), "roll": self.part(y, x, core)}

    def around_z(self, dz):
        return lax.rem(self.z + dz, self.zs)

    def across(self, steps):
        ways = [(dy, dx, dk) for dy in steps for dx in range(self.xs) for dk in range(2)]
        ways.sort(key=lambda w: -(min(w[0] % RING, -w[0] % RING) + min(w[1], self.xs - w[1])))
        return [
            (way, self.turn(way[0]), lax.rem(self.x + way[1], self.xs), lax.rem(self.core + way[2], 2))
            for way in ways
        ]

    def window(self, steps):
        ways = [(dy, dz) for dy in steps for dz in range(self.zs)]
        return sorted(ways, key=lambda w: -(abs(w[0]) + min(w[1], self.zs - w[1])))


def send(src, dst, sems, which, device):
    pltpu.make_async_remote_copy(
        src_ref=src,
        dst_ref=dst,
        send_sem=sems[0].at[which],
        recv_sem=sems[1].at[which],
        device_id=device,
        device_id_type=MESH,
    ).start()


def drain(part, sem):
    pltpu.make_async_copy(part, part, sem).wait()


def contract(left, right, dims):
    return lax.dot_general(left, right, (dims, ((), ())), preferred_element_type=F32)


def kernel(
    ctx,
    roll,
    order_hbm,
    seg_hbm,
    x_hbm,
    q_hbm,
    k_hbm,
    v_hbm,
    do_hbm,
    mw_hbm,
    m1_hbm,
    m2_hbm,
    qg_out,
    kvg_out,
    mw_out,
    m1_out,
    m2_out,
    rw_out,
    order,
    seg,
    x_in,
    q_in,
    k_in,
    v_in,
    do_in,
    state_in,
    state,
    state_new,
    kv_wide,
    bias,
    expo,
    dprob,
    kv,
    kv_other,
    tops,
    stats,
    dkv_to,
    dkv_from,
    dq_to,
    dq_near,
    dq_half,
    dq_from,
    dq_side,
    kvg,
    kvg_own,
    wg_to,
    wg_from,
    rolled_own,
    kvg_stage,
    load_sem,
    send_sem,
    recv_sem,
    out_sem,
):
    at = Place(ctx, roll)
    c, r = at.c, at.r
    sems = (send_sem, recv_sem)
    rows = k_in.shape[0]
    hd = k_in.shape[1]
    keys = ctx * SHARE
    scale = hd**-0.5
    piece = HEADS * SHARE
    zs = at.zs
    most = pl.ds(0, ctx - 1)
    others = pl.ds(0, roll - 1)

    class_home = [
        lax.rem(at.y + RING - lax.rem(at.y + RING - j, RUN), RING) for j in range(RUN)
    ]
    class_part = [at.part(home) for home in class_home]

    pairs = [(k_hbm, k_in), (v_hbm, v_in), (order_hbm, order), (seg_hbm, seg)]
    pairs += [(src, state_in.at[i]) for i, src in enumerate((mw_hbm, m1_hbm, m2_hbm))]
    pairs += [(q_hbm, q_in), (do_hbm, do_in)]
    pairs += [
        (x_hbm.at[pl.ds(j * zs, zs), class_part[j]], x_in.at[pl.ds(j * zs, zs)]) for j in range(RUN)
    ]
    loads = [
        pltpu.make_async_copy(src, dst, load_sem.at[i]) for i, (src, dst) in enumerate(pairs)
    ]
    for load in loads[:2]:
        load.start()

    barrier = pltpu.get_barrier_semaphore()
    greeted = 0

    def greet(device):
        pl.semaphore_signal(barrier, inc=1, device_id=device, device_id_type=MESH)

    for dy, dz in at.window((1, 0, -1, -2)):
        if (dy, dz) != (0, 0):
            greet(at.device(at.turn(dy), at.around_z(dz)))
            greeted += 1
    for way, y, x, core in at.across((2, -2, 0, 4)):
        if way not in ((0, 0, 0), (-2, 0, 0)):
            greet(at.device(y, at.z, x, core))
            greeted += 1

    for load in loads[2:]:
        load.start()

    loads[0].wait()
    loads[1].wait()
    kv_wide[0] = k_in[...].astype(F32)
    kv_wide[1] = v_in[...].astype(F32)

    def chunk(part):
        first = pl.multiple_of(part * SHARE, SHARE)
        both = [kv_wide[i, pl.ds(first, SHARE), :] for i in range(2)]
        return jnp.concatenate(both, axis=0).astype(BF)

    kv[c] = chunk(r)
    kv_other[...] = chunk(at.part(at.turn(4)))
    pl.semaphore_wait(barrier, greeted)
    for dy, dz in at.window((2, 1, 0, -1)):
        if (dy, dz) != (0, 0):
            src = kv_other if dy == -1 else kv.at[c]
            send(src, kv.at[c], sems, KV, at.device(at.turn(dy), at.around_z(dz)))
    for i in (4, 5, 6):
        loads[i].wait()
    send(state_in, state, sems, STATE, at.device(at.turn(2), at.z))

    loads[2].wait()
    loads[3].wait()
    ids = seg[...]
    q_seg = seg[pl.ds(c, 1), :]
    lane = lax.broadcasted_iota(jnp.int32, (1, rows), 1)
    q_pos = order[c] * rows + lane
    start = jnp.zeros((1, rows), F32)
    for rollout in range(3):
        total = jnp.sum(jnp.where(ids == rollout, 1.0, 0.0), axis=0, keepdims=True)
        total = jnp.sum(total, axis=1, keepdims=True)
        start = start + jnp.where(q_seg > rollout, total, 0.0)
    start = start.astype(jnp.int32)
    sub = lax.broadcasted_iota(jnp.int32, (SHARE, rows), 0)
    latest = q_pos - sub
    earliest = start - sub
    for block in range(ctx):
        base = order[block] * rows + class_part[block // zs] * SHARE
        seen = (latest >= base) & (earliest <= base)
        bias[pl.ds(block * SHARE, SHARE), :] = jnp.where(seen, 0.0, NEG_FILL)

    loads[7].wait()
    loads[8].wait()
    heads = [pl.ds(h * hd, hd) for h in range(HEADS)]
    lanes = [pl.ds(h * rows, rows) for h in range(HEADS)]
    q_rows = jnp.concatenate([q_in[:, cols] for cols in heads], axis=0)
    do_rows = jnp.concatenate([do_in[:, cols] for cols in heads], axis=0)
    drain(kv.at[most], recv_sem.at[KV])
    wide = kv[...].astype(F32)
    key = wide[:, :SHARE, :].reshape(keys, hd).astype(BF)
    value = wide[:, SHARE:, :].reshape(keys, hd).astype(BF)
    expo[...] = contract(key, q_rows, ((1,), (1,)))
    dprob[...] = contract(value, do_rows, ((1,), (1,)))
    for h in range(HEADS):
        scores = expo[:, lanes[h]] * scale + bias[...]
        top = jnp.max(scores, axis=0, keepdims=True)
        weights = jnp.exp(scores - top)
        expo[:, lanes[h]] = weights
        total = jnp.sum(weights, axis=0, keepdims=True)
        tops[h : h + 1] = top
        stats[r, 0, h : h + 1] = top + jnp.log(total)
        stats[r, 1, h : h + 1] = (
            jnp.sum(weights * dprob[:, lanes[h]], axis=0, keepdims=True) / total
        )
    tops[HEADS:] = jnp.zeros((8 - HEADS, rows), F32)
    for i in range(2):
        stats[r, i, HEADS:] = jnp.zeros((8 - HEADS, rows), F32)
    for way, y, x, core in at.across((4, 0)):
        if way != (0, 0, 0):
            send(stats.at[r], stats.at[r], sems, STATS, at.device(y, at.z, x, core))
    drain(stats.at[others], recv_sem.at[STATS])
    top = jnp.max(stats[:, 0], axis=0)
    factor = jnp.exp(stats[:, 0] - top[None])
    total = jnp.sum(factor, axis=0)
    delta = jnp.sum(stats[:, 1] * factor, axis=0) / total
    norm = jnp.exp(tops[...] - top) / total

    probs, dscores = [], []
    for h in range(HEADS):
        prob = expo[:, lanes[h]] * norm[h : h + 1]
        dscores.append((prob * (dprob[:, lanes[h]] - delta[h : h + 1])).astype(BF))
        probs.append(prob.astype(BF))
    dscore = jnp.concatenate(dscores, axis=1)
    key_grad = contract(dscore, q_rows, ((1,), (0,))) * scale
    value_grad = contract(jnp.concatenate(probs, axis=1), do_rows, ((1,), (0,)))
    both = jnp.concatenate(
        [key_grad.reshape(ctx, SHARE, hd), value_grad.reshape(ctx, SHARE, hd)], axis=1
    )
    dkv_to[...] = both.astype(BF)

    back = at.turn(-2)
    back_block = at.block(back, at.z)
    back_part = at.part(back)

    def scatter(to, arrived, which):
        for dy, dz in at.window((2, 1, 0, -1)):
            z = at.around_z(dz)
            if (dy, dz) != (0, 0):
                home = at.block(at.turn(dy - 2), z)
                send(to.at[home], arrived.at[c], sems, which, at.device(at.turn(dy), z))
        arrived[c] = to[back_block]

    scatter(dkv_to, dkv_from, DKV)

    drain(dkv_from.at[most], recv_sem.at[DKV])
    kvg_own[...] = jnp.sum(dkv_from[...].astype(F32), axis=0).astype(BF)

    def spread(own, arrived, which):
        for _, y, x, core in at.across((2, -2)):
            send(own, arrived.at[back_part], sems, which, at.device(y, at.z, x, core))

    spread(kvg_own, kvg, KVG)

    dq_to[...] = contract(dscore, key, ((0,), (0,))).astype(BF)
    sibling = at.device(at.y, at.z, at.x, 1 - at.core)
    side = dq_half.shape[0]

    def half(core):
        return pl.ds(pl.multiple_of(core * side, 16), side)

    def slot(y, x):
        return x * 2 + lax.div(y, RUN)

    def dq_piece(number):
        return pl.ds(pl.multiple_of(number * piece, 16), piece)

    mine = slot(at.y, at.x)
    chips = [(y, x) for way, y, x, _ in at.across((4, 0)) if way[2] == 0 and way != (0, 0, 0)]
    send(dq_to.at[half(1 - at.core)], dq_near, sems, PAIR, sibling)
    drain(dq_near, recv_sem.at[PAIR])
    dq_half[...] = (dq_to[half(at.core)].astype(F32) + dq_near[...].astype(F32)).astype(BF)
    for y, x in chips:
        send(dq_half.at[dq_piece(slot(y, x))], dq_from.at[mine], sems, DQ, at.device(y, at.z, x))
    dq_from[mine] = dq_half[dq_piece(mine)]

    for load in loads[9:]:
        load.wait()
    drain(kvg, recv_sem.at[KVG])
    wide = kvg[...].astype(F32)
    kv_wide[0] = wide[:, :SHARE, :].reshape(rows, hd)
    kv_wide[1] = wide[:, SHARE:, :].reshape(rows, hd)
    key_grad = kv_wide[0].astype(BF)
    product = contract(x_in[...].reshape(ctx * OWN, rows), key_grad, ((1,), (0,)))
    wg_to[...] = product.astype(BF).reshape(ctx, OWN, hd)
    scatter(wg_to, wg_from, WG)

    kvg_stage[:, :hd] = key_grad
    kvg_stage[:, hd:] = kv_wide[1].astype(BF)
    outs = []

    def put(src, dst):
        outs.append(pltpu.make_async_copy(src, dst, out_sem.at[len(outs)]))
        outs[-1].start()

    put(kvg_stage, kvg_out)
    drain(dq_from.at[pl.ds(0, len(chips))], recv_sem.at[DQ])
    dq_side[dq_piece(mine)] = (jnp.sum(dq_from[...].astype(F32), axis=0) * scale).astype(BF)
    summed = dq_side.at[dq_piece(mine)]
    for y, x in chips:
        send(summed, summed, sems, DQALL, at.device(y, at.z, x))

    drain(state, recv_sem.at[STATE])
    drain(wg_from.at[most], recv_sem.at[WG])
    grad = jnp.sum(wg_from[...].astype(F32), axis=0)
    master = state[0]
    new_first = BETA_ONE * state[1] + (1.0 - BETA_ONE) * grad
    new_second = BETA_TWO * state[2] + (1.0 - BETA_TWO) * grad * grad
    update = (
        new_first / CORRECT_ONE / (jnp.sqrt(new_second / CORRECT_TWO) + ADAM_EPS)
        + DECAY_RATE * master
    )
    new_master = master - LEARN_RATE * update
    rolled_own[...] = new_master.astype(BF)
    spread(rolled_own, rw_out, ROLL)
    state_new[0] = new_master
    state_new[1] = new_first
    state_new[2] = new_second
    for i, out in enumerate((mw_out, m1_out, m2_out)):
        send(state_new.at[i], out, sems, BACK, at.device(back, at.z))

    dq_most = pl.ds(0, len(chips) * piece)
    drain(dq_side.at[dq_most], recv_sem.at[DQALL])
    send(dq_side, qg_out.at[half(at.core)], sems, GIVE, sibling)
    put(dq_side, qg_out.at[half(at.core)])
    drain(kv.at[most], send_sem.at[KV])
    drain(state_in, send_sem.at[STATE])
    drain(stats.at[others], send_sem.at[STATS])
    drain(dkv_to.at[most], send_sem.at[DKV])
    drain(dq_near, send_sem.at[PAIR])
    drain(dq_side.at[dq_most], send_sem.at[DQ])
    drain(kvg, send_sem.at[KVG])
    drain(wg_to.at[most], send_sem.at[WG])
    drain(dq_side.at[dq_most], send_sem.at[DQALL])
    drain(dq_side, send_sem.at[GIVE])
    drain(kvg, send_sem.at[ROLL])
    drain(state_new, send_sem.at[BACK])
    drain(state_new, recv_sem.at[BACK])
    drain(dq_side, recv_sem.at[GIVE])
    drain(kvg, recv_sem.at[ROLL])
    for out in outs:
        out.wait()


def hand_over(*refs):
    sources, places, held, sem = refs[:6], refs[6:12], refs[12:18], refs[18]
    rows, hd = places[0].shape[0], sources[0].shape[1]
    pairs = [(i, src, held[i]) for i, src in enumerate(sources)][1:]
    pairs += [
        (0, sources[0].at[pl.ds(h * rows, rows)], held[0].at[:, pl.ds(h * hd, hd)])
        for h in range(HEADS)
    ]
    fetches = [
        (i, pltpu.make_async_copy(src, dst, sem.at[0, n])) for n, (i, src, dst) in enumerate(pairs)
    ]
    writes = [
        pltpu.make_async_copy(src, dst, sem.at[1, i])
        for i, (src, dst) in enumerate(zip(held, places))
    ]
    for _, fetch in fetches:
        fetch.start()
    for i, fetch in fetches:
        fetch.wait()
        if i > 0:
            writes[i].start()
    writes[0].start()
    for write in writes:
        write.wait()


def body(order, segments, layer_input, query, key, value, out_grad, master, first, second):
    ctx = lax.axis_size("ctx")
    roll = lax.axis_size("roll")
    rows, hd = key.shape
    width = query.shape[1]
    keys = ctx * SHARE
    piece = HEADS * SHARE
    shape = jax.ShapeDtypeStruct
    vmem = pltpu.VMEM
    anywhere = pl.BlockSpec(memory_space=pl.ANY)
    shapes = (
        shape((rows, width), BF),
        shape((rows, 2 * hd), BF),
        shape((OWN, hd), F32),
        shape((OWN, hd), F32),
        shape((OWN, hd), F32),
        shape((roll, OWN, hd), BF),
    )
    made = pl.pallas_call(
        functools.partial(kernel, ctx, roll),
        out_shape=(shape((HEADS * rows, hd), BF), *shapes[1:]),
        in_specs=[anywhere] * 10,
        out_specs=[anywhere] * 6,
        scratch_shapes=[
            pltpu.SMEM((ctx,), jnp.int32),
            vmem((ctx, rows), jnp.int32),
            vmem((ctx, OWN, rows), BF),
            vmem((rows, width), BF),
            vmem((rows, hd), BF),
            vmem((rows, hd), BF),
            vmem((rows, width), BF),
            vmem((3, OWN, hd), F32),
            vmem((3, OWN, hd), F32),
            vmem((3, OWN, hd), F32),
            vmem((2, rows, hd), F32),
            vmem((keys, rows), F32),
            vmem((keys, HEADS * rows), F32),
            vmem((keys, HEADS * rows), F32),
            vmem((ctx, 2 * SHARE, hd), BF),
            vmem((2 * SHARE, hd), BF),
            vmem((8, rows), F32),
            vmem((roll, 2, 8, rows), F32),
            vmem((ctx, 2 * SHARE, hd), BF),
            vmem((ctx, 2 * SHARE, hd), BF),
            vmem((roll * piece, hd), BF),
            vmem((roll // 2 * piece, hd), BF),
            vmem((roll // 2 * piece, hd), BF),
            vmem((roll // 2, piece, hd), BF),
            vmem((roll // 2 * piece, hd), BF),
            vmem((roll, 2 * SHARE, hd), BF),
            vmem((2 * SHARE, hd), BF),
            vmem((ctx, OWN, hd), BF),
            vmem((ctx, OWN, hd), BF),
            vmem((OWN, hd), BF),
            vmem((rows, 2 * hd), BF),
            pltpu.SemaphoreType.DMA((13,)),
            pltpu.SemaphoreType.DMA((12,)),
            pltpu.SemaphoreType.DMA((12,)),
            pltpu.SemaphoreType.DMA((12,)),
        ],
        compiler_params=pltpu.CompilerParams(
            collective_id=0, has_side_effects=True, vmem_limit_bytes=56 * 1024 * 1024
        ),
    )(
        order,
        segments.reshape(ctx, rows),
        layer_input.reshape(ctx, roll, OWN, rows),
        query,
        key,
        value,
        out_grad,
        master,
        first,
        second,
    )
    query_grad, key_value, new_master, new_first, new_second, rolled = pl.pallas_call(
        hand_over,
        out_shape=shapes,
        in_specs=[anywhere] * 6,
        out_specs=[anywhere] * 6,
        scratch_shapes=[*(vmem(s.shape, s.dtype) for s in shapes), pltpu.SemaphoreType.DMA((2, 11))],
    )(*made)
    return (
        query_grad,
        key_value,
        new_master,
        new_first,
        new_second,
        rolled.reshape(roll * OWN, hd),
    )


def solution(mesh):
    placed = (
        P(),
        P(),
        P(None, "ctx"),
        P("ctx", None),
        P("ctx", None),
        P("ctx", None),
        P("ctx", None),
        P(("ctx", "roll"), None),
        P(("ctx", "roll"), None),
        P(("ctx", "roll"), None),
    )
    return jax.shard_map(
        body,
        mesh=mesh,
        in_specs=placed,
        out_specs=(
            P("ctx", None),
            P("ctx", None),
            P(("ctx", "roll"), None),
            P(("ctx", "roll"), None),
            P(("ctx", "roll"), None),
            P("ctx", None),
        ),
        check_vma=False,
    )
```

```python
import functools

import jax
import jax.numpy as jnp
from jax import lax
from jax.experimental import pallas as pl
from jax.experimental.pallas import tpu as pltpu
from jax.sharding import PartitionSpec as P

NEG_FILL = -1e30
BETA_ONE = 0.9
BETA_TWO = 0.95
ADAM_EPS = 1e-08
DECAY_RATE = 0.1
LEARN_RATE = 1e-06
CORRECT_ONE = 0.9999734386011124
CORRECT_TWO = 0.994079470779666

MESH = pl.DeviceIdType.MESH
RING = 8
RUN = 4
SHARE = 8
OWN = 16
HEADS = 6
BF = jnp.bfloat16
F32 = jnp.float32

(KV, STATE, STATS, DKV, PAIR, DQ, DQALL, GIVE, KVG, WG, ROLL, BACK) = range(12)


class Place:
    def __init__(self, ctx, roll):
        self.zs, self.xs = ctx // RUN, roll // (2 * (RING // RUN))
        self.c, self.r = lax.axis_index("ctx"), lax.axis_index("roll")
        self.z = lax.rem(self.c, self.zs)
        self.x = lax.div(self.r, 4)
        self.core = lax.rem(self.r, 2)
        self.y = lax.div(self.c, self.zs) + RUN * lax.rem(lax.div(self.r, 2), 2)

    def turn(self, dy):
        return lax.rem(self.y + (dy + RING), RING)

    def block(self, y, z):
        return lax.rem(y, RUN) * self.zs + z

    def part(self, y, x=None, core=None):
        x = self.x if x is None else x
        core = self.core if core is None else core
        return x * 4 + lax.div(y, RUN) * 2 + core

    def device(self, y, z, x=None, core=None):
        return {"ctx": self.block(y, z), "roll": self.part(y, x, core)}

    def around_z(self, dz):
        return lax.rem(self.z + dz, self.zs)

    def across(self, steps):
        ways = [(dy, dx, dk) for dy in steps for dx in range(self.xs) for dk in range(2)]
        ways.sort(key=lambda w: -(min(w[0] % RING, -w[0] % RING) + min(w[1], self.xs - w[1])))
        return [
            (way, self.turn(way[0]), lax.rem(self.x + way[1], self.xs), lax.rem(self.core + way[2], 2))
            for way in ways
        ]

    def window(self, steps):
        ways = [(dy, dz) for dy in steps for dz in range(self.zs)]
        return sorted(ways, key=lambda w: -(abs(w[0]) + min(w[1], self.zs - w[1])))


def send(src, dst, sems, which, device):
    pltpu.make_async_remote_copy(
        src_ref=src,
        dst_ref=dst,
        send_sem=sems[0].at[which],
        recv_sem=sems[1].at[which],
        device_id=device,
        device_id_type=MESH,
    ).start()


def drain(part, sem):
    pltpu.make_async_copy(part, part, sem).wait()


def stepped(state, grad):
    master = state[0]
    new_first = BETA_ONE * state[1] + (1.0 - BETA_ONE) * grad
    new_second = BETA_TWO * state[2] + (1.0 - BETA_TWO) * grad * grad
    update = (
        new_first / CORRECT_ONE / (jnp.sqrt(new_second / CORRECT_TWO) + ADAM_EPS)
        + DECAY_RATE * master
    )
    return master - LEARN_RATE * update, new_first, new_second


def contract(left, right, dims):
    return lax.dot_general(left, right, (dims, ((), ())), preferred_element_type=F32)


def kernel(
    ctx,
    roll,
    order_hbm,
    seg_hbm,
    x_hbm,
    q_hbm,
    k_hbm,
    v_hbm,
    do_hbm,
    mw_hbm,
    m1_hbm,
    m2_hbm,
    qg_out,
    kvg_out,
    mw_out,
    m1_out,
    m2_out,
    rw_out,
    order,
    seg,
    x_in,
    q_in,
    k_in,
    v_in,
    do_in,
    state_in,
    state,
    state_new,
    grad_own,
    grad_back,
    kv_wide,
    bias,
    expo,
    dprob,
    kv,
    kv_other,
    tops,
    stats,
    dkv_to,
    dkv_from,
    dq_to,
    dq_near,
    dq_half,
    dq_from,
    dq_side,
    kvg,
    kvg_own,
    wg_to,
    wg_from,
    rolled_own,
    kvg_stage,
    load_sem,
    send_sem,
    recv_sem,
    out_sem,
):
    at = Place(ctx, roll)
    c, r = at.c, at.r
    sems = (send_sem, recv_sem)
    rows = k_in.shape[0]
    hd = k_in.shape[1]
    keys = ctx * SHARE
    scale = hd**-0.5
    piece = HEADS * SHARE
    zs = at.zs
    most = pl.ds(0, ctx - 1)
    others = pl.ds(0, roll - 1)

    ways = at.window((2, 1, 0, -1))
    at_way = {way: n for n, way in enumerate(ways)}
    homes = [(at.turn(dy - 2), at.around_z(dz)) for dy, dz in ways]
    blocks = [at.block(y, z) for y, z in homes]
    own_slot = at_way[2, 0]
    last = len(ways) - 1

    class_home = [
        lax.rem(at.y + RING - lax.rem(at.y + RING - j, RUN), RING) for j in range(RUN)
    ]
    class_part = [at.part(home) for home in class_home]

    pairs = [(k_hbm, k_in), (v_hbm, v_in), (order_hbm, order), (seg_hbm, seg)]
    pairs += [(src, state_in.at[i]) for i, src in enumerate((mw_hbm, m1_hbm, m2_hbm))]
    pairs += [(q_hbm, q_in), (do_hbm, do_in)]
    pairs += [
        (x_hbm.at[pl.ds(j * zs, zs), class_part[j]], x_in.at[pl.ds(j * zs, zs)]) for j in range(RUN)
    ]
    loads = [
        pltpu.make_async_copy(src, dst, load_sem.at[i]) for i, (src, dst) in enumerate(pairs)
    ]
    for load in loads[:2]:
        load.start()

    barrier = pltpu.get_barrier_semaphore()
    greeted = 0

    def greet(device):
        pl.semaphore_signal(barrier, inc=1, device_id=device, device_id_type=MESH)

    for dy, dz in at.window((1, 0, -1, -2)):
        if (dy, dz) != (0, 0):
            greet(at.device(at.turn(dy), at.around_z(dz)))
            greeted += 1
    for way, y, x, core in at.across((2, -2, 0, 4)):
        if way not in ((0, 0, 0), (-2, 0, 0)):
            greet(at.device(y, at.z, x, core))
            greeted += 1

    loads[0].wait()
    loads[1].wait()
    kv_wide[0] = k_in[...].astype(F32)
    kv_wide[1] = v_in[...].astype(F32)

    def chunk(part):
        first = pl.multiple_of(part * SHARE, SHARE)
        both = [kv_wide[i, pl.ds(first, SHARE), :] for i in range(2)]
        return jnp.concatenate(both, axis=0).astype(BF)

    kv[own_slot] = chunk(r)
    kv_other[...] = chunk(at.part(at.turn(4)))
    pl.semaphore_wait(barrier, greeted)
    for dy, dz in ways:
        if (dy, dz) != (0, 0):
            src = kv_other if dy == -1 else kv.at[own_slot]
            there = at_way[-1 if dy == -1 else 2 - dy, -dz % zs]
            send(src, kv.at[there], sems, KV, at.device(at.turn(dy), at.around_z(dz)))
    for load in loads[2:]:
        load.start()
    for i in (4, 5, 6):
        loads[i].wait()
    send(state_in, state, sems, STATE, at.device(at.turn(2), at.z))

    loads[2].wait()
    loads[3].wait()
    ids = seg[...]
    q_seg = seg[pl.ds(c, 1), :]
    lane = lax.broadcasted_iota(jnp.int32, (1, rows), 1)
    q_pos = order[c] * rows + lane
    start = jnp.zeros((1, rows), F32)
    for rollout in range(3):
        total = jnp.sum(jnp.where(ids == rollout, 1.0, 0.0), axis=0, keepdims=True)
        total = jnp.sum(total, axis=1, keepdims=True)
        start = start + jnp.where(q_seg > rollout, total, 0.0)
    start = start.astype(jnp.int32)
    sub = lax.broadcasted_iota(jnp.int32, (SHARE, rows), 0)
    latest = q_pos - sub
    earliest = start - sub
    for n in range(ctx):
        base = order[blocks[n]] * rows + at.part(homes[n][0]) * SHARE
        seen = (latest >= base) & (earliest <= base)
        bias[pl.ds(n * SHARE, SHARE), :] = jnp.where(seen, 0.0, NEG_FILL)

    loads[7].wait()
    loads[8].wait()
    heads = [pl.ds(h * hd, hd) for h in range(HEADS)]
    lanes = [pl.ds(h * rows, rows) for h in range(HEADS)]
    q_rows = jnp.concatenate([q_in[:, cols] for cols in heads], axis=0)
    do_rows = jnp.concatenate([do_in[:, cols] for cols in heads], axis=0)
    drain(kv.at[most], recv_sem.at[KV])
    wide = kv[...].astype(F32)
    key = wide[:, :SHARE, :].reshape(keys, hd).astype(BF)
    value = wide[:, SHARE:, :].reshape(keys, hd).astype(BF)
    expo[...] = contract(key, q_rows, ((1,), (1,)))
    dprob[...] = contract(value, do_rows, ((1,), (1,)))
    for h in range(HEADS):
        scores = expo[:, lanes[h]] * scale + bias[...]
        top = jnp.max(scores, axis=0, keepdims=True)
        weights = jnp.exp(scores - top)
        expo[:, lanes[h]] = weights
        total = jnp.sum(weights, axis=0, keepdims=True)
        tops[h : h + 1] = top
        stats[r, 0, h : h + 1] = top + jnp.log(total)
        stats[r, 1, h : h + 1] = (
            jnp.sum(weights * dprob[:, lanes[h]], axis=0, keepdims=True) / total
        )
    tops[HEADS:] = jnp.zeros((8 - HEADS, rows), F32)
    for i in range(2):
        stats[r, i, HEADS:] = jnp.zeros((8 - HEADS, rows), F32)
    for way, y, x, core in at.across((4, 0)):
        if way != (0, 0, 0):
            send(stats.at[r], stats.at[r], sems, STATS, at.device(y, at.z, x, core))
    drain(stats.at[others], recv_sem.at[STATS])
    top = jnp.max(stats[:, 0], axis=0)
    factor = jnp.exp(stats[:, 0] - top[None])
    total = jnp.sum(factor, axis=0)
    delta = jnp.sum(stats[:, 1] * factor, axis=0) / total
    norm = jnp.exp(tops[...] - top) / total

    back = at.turn(-2)
    back_block = at.block(back, at.z)
    back_part = at.part(back)
    halves = [range(0, ctx // 2), range(ctx // 2, ctx)]

    def scatter(part, to, arrived, which):
        for n in part:
            if n < last:
                dy, dz = ways[n]
                device = at.device(at.turn(dy), at.around_z(dz))
                send(to.at[n], arrived.at[n], sems, which, device)

    dscores = []
    for part in halves:
        span = pl.ds(part[0] * SHARE, keys // 2)
        slots = pl.ds(part[0], ctx // 2)
        probs, scored = [], []
        for h in range(HEADS):
            prob = expo[span, lanes[h]] * norm[h : h + 1]
            scored.append((prob * (dprob[span, lanes[h]] - delta[h : h + 1])).astype(BF))
            probs.append(prob.astype(BF))
        dscores.append(jnp.concatenate(scored, axis=1))
        key_grad = contract(dscores[-1], q_rows, ((1,), (0,))) * scale
        value_grad = contract(jnp.concatenate(probs, axis=1), do_rows, ((1,), (0,)))
        both = [g.reshape(ctx // 2, SHARE, hd) for g in (key_grad, value_grad)]
        dkv_to[slots] = jnp.concatenate(both, axis=1).astype(BF)
        scatter(part, dkv_to, dkv_from, DKV)
    dkv_from[last] = dkv_to[last]

    drain(dkv_from.at[most], recv_sem.at[DKV])
    kvg_own[...] = jnp.sum(dkv_from[...].astype(F32), axis=0).astype(BF)

    def spread(own, arrived, which):
        for _, y, x, core in at.across((2, -2)):
            send(own, arrived.at[back_part], sems, which, at.device(y, at.z, x, core))

    spread(kvg_own, kvg, KVG)

    dscore = jnp.concatenate(dscores, axis=0)
    dq_to[...] = contract(dscore, key, ((0,), (0,))).astype(BF)
    sibling = at.device(at.y, at.z, at.x, 1 - at.core)
    side = dq_half.shape[0]

    def half(core):
        return pl.ds(pl.multiple_of(core * side, 16), side)

    def slot(y, x):
        return x * 2 + lax.div(y, RUN)

    def dq_piece(number):
        return pl.ds(pl.multiple_of(number * piece, 16), piece)

    mine = slot(at.y, at.x)
    chips = [(y, x) for way, y, x, _ in at.across((4, 0)) if way[2] == 0 and way != (0, 0, 0)]
    send(dq_to.at[half(1 - at.core)], dq_near, sems, PAIR, sibling)
    drain(dq_near, recv_sem.at[PAIR])
    dq_half[...] = (dq_to[half(at.core)].astype(F32) + dq_near[...].astype(F32)).astype(BF)
    for y, x in chips:
        send(dq_half.at[dq_piece(slot(y, x))], dq_from.at[mine], sems, DQ, at.device(y, at.z, x))
    dq_from[mine] = dq_half[dq_piece(mine)]

    for load in loads[9:]:
        load.wait()
    drain(kvg, recv_sem.at[KVG])
    wide = kvg[...].astype(F32)
    kv_wide[0] = wide[:, :SHARE, :].reshape(rows, hd)
    kv_wide[1] = wide[:, SHARE:, :].reshape(rows, hd)
    key_grad = kv_wide[0].astype(BF)
    for part in halves:
        taken = jnp.concatenate([x_in[blocks[n]] for n in part], axis=0)
        product = contract(taken, key_grad, ((1,), (0,)))
        wg_to[pl.ds(part[0], ctx // 2)] = product.astype(BF).reshape(ctx // 2, OWN, hd)
        scatter(part, wg_to, wg_from, WG)
    wg_from[last] = wg_to[last]

    kvg_stage[:, :hd] = key_grad
    kvg_stage[:, hd:] = kv_wide[1].astype(BF)
    outs = []

    def put(src, dst):
        outs.append(pltpu.make_async_copy(src, dst, out_sem.at[len(outs)]))
        outs[-1].start()

    put(kvg_stage, kvg_out)
    drain(dq_from.at[pl.ds(0, len(chips))], recv_sem.at[DQ])
    dq_side[dq_piece(mine)] = (jnp.sum(dq_from[...].astype(F32), axis=0) * scale).astype(BF)
    summed = dq_side.at[dq_piece(mine)]
    for y, x in chips:
        send(summed, summed, sems, DQALL, at.device(y, at.z, x))

    drain(state, recv_sem.at[STATE])
    drain(wg_from.at[most], recv_sem.at[WG])
    grad_own[...] = jnp.sum(wg_from[...].astype(F32), axis=0)
    send(grad_own, grad_back, sems, BACK, at.device(back, at.z))
    rolled_own[...] = stepped(state, grad_own[...])[0].astype(BF)
    spread(rolled_own, rw_out, ROLL)

    drain(grad_back, recv_sem.at[BACK])
    for i, (new, out) in enumerate(
        zip(stepped(state_in, grad_back[...]), (mw_out, m1_out, m2_out))
    ):
        state_new[i] = new
        put(state_new.at[i], out)

    dq_most = pl.ds(0, len(chips) * piece)
    drain(dq_side.at[dq_most], recv_sem.at[DQALL])
    send(dq_side, qg_out.at[half(at.core)], sems, GIVE, sibling)
    put(dq_side, qg_out.at[half(at.core)])
    drain(kv.at[most], send_sem.at[KV])
    drain(state_in, send_sem.at[STATE])
    drain(stats.at[others], send_sem.at[STATS])
    drain(dkv_to.at[most], send_sem.at[DKV])
    drain(dq_near, send_sem.at[PAIR])
    drain(dq_side.at[dq_most], send_sem.at[DQ])
    drain(kvg, send_sem.at[KVG])
    drain(wg_to.at[most], send_sem.at[WG])
    drain(dq_side.at[dq_most], send_sem.at[DQALL])
    drain(dq_side, send_sem.at[GIVE])
    drain(kvg, send_sem.at[ROLL])
    drain(grad_own, send_sem.at[BACK])
    drain(dq_side, recv_sem.at[GIVE])
    drain(kvg, recv_sem.at[ROLL])
    for out in outs:
        out.wait()


def hand_over(*refs):
    sources, places, held, sem = refs[:6], refs[6:12], refs[12:18], refs[18]
    rows, hd = places[0].shape[0], sources[0].shape[1]
    pairs = [(i, src, held[i]) for i, src in enumerate(sources)][1:]
    pairs += [
        (0, sources[0].at[pl.ds(h * rows, rows)], held[0].at[:, pl.ds(h * hd, hd)])
        for h in range(HEADS)
    ]
    fetches = [
        (i, pltpu.make_async_copy(src, dst, sem.at[0, n])) for n, (i, src, dst) in enumerate(pairs)
    ]
    writes = [
        pltpu.make_async_copy(src, dst, sem.at[1, i])
        for i, (src, dst) in enumerate(zip(held, places))
    ]
    for _, fetch in fetches:
        fetch.start()
    for i, fetch in fetches:
        fetch.wait()
        if i > 0:
            writes[i].start()
    writes[0].start()
    for write in writes:
        write.wait()


def body(order, segments, layer_input, query, key, value, out_grad, master, first, second):
    ctx = lax.axis_size("ctx")
    roll = lax.axis_size("roll")
    rows, hd = key.shape
    width = query.shape[1]
    keys = ctx * SHARE
    piece = HEADS * SHARE
    shape = jax.ShapeDtypeStruct
    vmem = pltpu.VMEM
    anywhere = pl.BlockSpec(memory_space=pl.ANY)
    shapes = (
        shape((rows, width), BF),
        shape((rows, 2 * hd), BF),
        shape((OWN, hd), F32),
        shape((OWN, hd), F32),
        shape((OWN, hd), F32),
        shape((roll, OWN, hd), BF),
    )
    made = pl.pallas_call(
        functools.partial(kernel, ctx, roll),
        out_shape=(shape((HEADS * rows, hd), BF), *shapes[1:]),
        in_specs=[anywhere] * 10,
        out_specs=[anywhere] * 6,
        scratch_shapes=[
            pltpu.SMEM((ctx,), jnp.int32),
            vmem((ctx, rows), jnp.int32),
            vmem((ctx, OWN, rows), BF),
            vmem((rows, width), BF),
            vmem((rows, hd), BF),
            vmem((rows, hd), BF),
            vmem((rows, width), BF),
            vmem((3, OWN, hd), F32),
            vmem((3, OWN, hd), F32),
            vmem((3, OWN, hd), F32),
            vmem((OWN, hd), F32),
            vmem((OWN, hd), F32),
            vmem((2, rows, hd), F32),
            vmem((keys, rows), F32),
            vmem((keys, HEADS * rows), F32),
            vmem((keys, HEADS * rows), F32),
            vmem((ctx, 2 * SHARE, hd), BF),
            vmem((2 * SHARE, hd), BF),
            vmem((8, rows), F32),
            vmem((roll, 2, 8, rows), F32),
            vmem((ctx, 2 * SHARE, hd), BF),
            vmem((ctx, 2 * SHARE, hd), BF),
            vmem((roll * piece, hd), BF),
            vmem((roll // 2 * piece, hd), BF),
            vmem((roll // 2 * piece, hd), BF),
            vmem((roll // 2, piece, hd), BF),
            vmem((roll // 2 * piece, hd), BF),
            vmem((roll, 2 * SHARE, hd), BF),
            vmem((2 * SHARE, hd), BF),
            vmem((ctx, OWN, hd), BF),
            vmem((ctx, OWN, hd), BF),
            vmem((OWN, hd), BF),
            vmem((rows, 2 * hd), BF),
            pltpu.SemaphoreType.DMA((13,)),
            pltpu.SemaphoreType.DMA((12,)),
            pltpu.SemaphoreType.DMA((12,)),
            pltpu.SemaphoreType.DMA((12,)),
        ],
        compiler_params=pltpu.CompilerParams(
            collective_id=0, has_side_effects=True, vmem_limit_bytes=56 * 1024 * 1024
        ),
    )(
        order,
        segments.reshape(ctx, rows),
        layer_input.reshape(ctx, roll, OWN, rows),
        query,
        key,
        value,
        out_grad,
        master,
        first,
        second,
    )
    query_grad, key_value, new_master, new_first, new_second, rolled = pl.pallas_call(
        hand_over,
        out_shape=shapes,
        in_specs=[anywhere] * 6,
        out_specs=[anywhere] * 6,
        scratch_shapes=[*(vmem(s.shape, s.dtype) for s in shapes), pltpu.SemaphoreType.DMA((2, 11))],
    )(*made)
    return (
        query_grad,
        key_value,
        new_master,
        new_first,
        new_second,
        rolled.reshape(roll * OWN, hd),
    )


def solution(mesh):
    placed = (
        P(),
        P(),
        P(None, "ctx"),
        P("ctx", None),
        P("ctx", None),
        P("ctx", None),
        P("ctx", None),
        P(("ctx", "roll"), None),
        P(("ctx", "roll"), None),
        P(("ctx", "roll"), None),
    )
    return jax.shard_map(
        body,
        mesh=mesh,
        in_specs=placed,
        out_specs=(
            P("ctx", None),
            P("ctx", None),
            P(("ctx", "roll"), None),
            P(("ctx", "roll"), None),
            P(("ctx", "roll"), None),
            P("ctx", None),
        ),
        check_vma=False,
    )
```

```python
import functools

import jax
import jax.numpy as jnp
from jax import lax
from jax.experimental import pallas as pl
from jax.experimental.pallas import tpu as pltpu
from jax.sharding import PartitionSpec as P

NEG_FILL = -1e30
BETA_ONE = 0.9
BETA_TWO = 0.95
ADAM_EPS = 1e-08
DECAY_RATE = 0.1
LEARN_RATE = 1e-06
CORRECT_ONE = 0.9999734386011124
CORRECT_TWO = 0.994079470779666

MESH = pl.DeviceIdType.MESH
RING = 8
RUN = 4
SHARE = 8
OWN = 16
HEADS = 6
BF = jnp.bfloat16
F32 = jnp.float32

(KV, STATE, STATS, DKV, PAIR, DQ, DQALL, GIVE, KVG, WG, ROLL, BACK) = range(12)


class Place:
    def __init__(self, ctx, roll):
        self.zs, self.xs = ctx // RUN, roll // (2 * (RING // RUN))
        self.c, self.r = lax.axis_index("ctx"), lax.axis_index("roll")
        self.z = lax.rem(self.c, self.zs)
        self.x = lax.div(self.r, 4)
        self.core = lax.rem(self.r, 2)
        self.y = lax.div(self.c, self.zs) + RUN * lax.rem(lax.div(self.r, 2), 2)

    def turn(self, dy):
        return lax.rem(self.y + (dy + RING), RING)

    def block(self, y, z):
        return lax.rem(y, RUN) * self.zs + z

    def part(self, y, x=None, core=None):
        x = self.x if x is None else x
        core = self.core if core is None else core
        return x * 4 + lax.div(y, RUN) * 2 + core

    def device(self, y, z, x=None, core=None):
        return {"ctx": self.block(y, z), "roll": self.part(y, x, core)}

    def around_z(self, dz):
        return lax.rem(self.z + dz, self.zs)

    def across(self, steps):
        ways = [(dy, dx, dk) for dy in steps for dx in range(self.xs) for dk in range(2)]
        ways.sort(key=lambda w: -(min(w[0] % RING, -w[0] % RING) + min(w[1], self.xs - w[1])))
        return [
            (way, self.turn(way[0]), lax.rem(self.x + way[1], self.xs), lax.rem(self.core + way[2], 2))
            for way in ways
        ]

    def window(self, steps):
        ways = [(dy, dz) for dy in steps for dz in range(self.zs)]
        return sorted(ways, key=lambda w: -(abs(w[0]) + min(w[1], self.zs - w[1])))


def send(src, dst, sems, which, device):
    pltpu.make_async_remote_copy(
        src_ref=src,
        dst_ref=dst,
        send_sem=sems[0].at[which],
        recv_sem=sems[1].at[which],
        device_id=device,
        device_id_type=MESH,
    ).start()


def drain(part, sem):
    pltpu.make_async_copy(part, part, sem).wait()


def contract(left, right, dims):
    return lax.dot_general(left, right, (dims, ((), ())), preferred_element_type=F32)


def kernel(
    ctx,
    roll,
    order_hbm,
    seg_hbm,
    x_hbm,
    q_hbm,
    k_hbm,
    v_hbm,
    do_hbm,
    mw_hbm,
    m1_hbm,
    m2_hbm,
    qg_out,
    kvg_out,
    mw_out,
    m1_out,
    m2_out,
    rw_out,
    order,
    seg,
    x_in,
    q_in,
    k_in,
    v_in,
    do_in,
    state_in,
    state,
    state_new,
    kv_wide,
    bias,
    expo,
    dprob,
    kv,
    kv_other,
    tops,
    stats,
    dkv_to,
    dkv_from,
    dq_to,
    dq_near,
    dq_half,
    dq_from,
    dq_side,
    kvg,
    kvg_own,
    wg_to,
    wg_from,
    rolled_own,
    kvg_stage,
    load_sem,
    send_sem,
    recv_sem,
    out_sem,
):
    at = Place(ctx, roll)
    c, r = at.c, at.r
    sems = (send_sem, recv_sem)
    rows = k_in.shape[0]
    hd = k_in.shape[1]
    keys = ctx * SHARE
    scale = hd**-0.5
    piece = HEADS * SHARE
    zs = at.zs
    most = pl.ds(0, ctx - 1)
    others = pl.ds(0, roll - 1)

    class_home = [
        lax.rem(at.y + RING - lax.rem(at.y + RING - j, RUN), RING) for j in range(RUN)
    ]
    class_part = [at.part(home) for home in class_home]

    pairs = [(k_hbm, k_in), (v_hbm, v_in), (order_hbm, order), (seg_hbm, seg)]
    pairs += [(src, state_in.at[i]) for i, src in enumerate((mw_hbm, m1_hbm, m2_hbm))]
    pairs += [(q_hbm, q_in), (do_hbm, do_in)]
    pairs += [
        (x_hbm.at[pl.ds(j * zs, zs), class_part[j]], x_in.at[pl.ds(j * zs, zs)]) for j in range(RUN)
    ]
    loads = [
        pltpu.make_async_copy(src, dst, load_sem.at[i]) for i, (src, dst) in enumerate(pairs)
    ]
    for load in loads[:2]:
        load.start()

    barrier = pltpu.get_barrier_semaphore()
    greeted = 0

    def greet(device):
        pl.semaphore_signal(barrier, inc=1, device_id=device, device_id_type=MESH)

    for dy, dz in at.window((1, 0, -1, -2)):
        if (dy, dz) != (0, 0):
            greet(at.device(at.turn(dy), at.around_z(dz)))
            greeted += 1
    for way, y, x, core in at.across((2, -2, 0, 4)):
        if way not in ((0, 0, 0), (-2, 0, 0)):
            greet(at.device(y, at.z, x, core))
            greeted += 1

    for load in loads[2:]:
        load.start()

    loads[0].wait()
    loads[1].wait()
    kv_wide[0] = k_in[...].astype(F32)
    kv_wide[1] = v_in[...].astype(F32)

    def chunk(part):
        first = pl.multiple_of(part * SHARE, SHARE)
        both = [kv_wide[i, pl.ds(first, SHARE), :] for i in range(2)]
        return jnp.concatenate(both, axis=0).astype(BF)

    kv[c] = chunk(r)
    kv_other[...] = chunk(at.part(at.turn(4)))
    pl.semaphore_wait(barrier, greeted)
    for dy, dz in at.window((2, 1, 0, -1)):
        if (dy, dz) != (0, 0):
            src = kv_other if dy == -1 else kv.at[c]
            send(src, kv.at[c], sems, KV, at.device(at.turn(dy), at.around_z(dz)))
    for i in (4, 5, 6):
        loads[i].wait()
    send(state_in, state, sems, STATE, at.device(at.turn(2), at.z))

    loads[2].wait()
    loads[3].wait()
    ids = seg[...]
    q_seg = seg[pl.ds(c, 1), :]
    lane = lax.broadcasted_iota(jnp.int32, (1, rows), 1)
    q_pos = order[c] * rows + lane
    start = jnp.zeros((1, rows), F32)
    for rollout in range(3):
        total = jnp.sum(jnp.where(ids == rollout, 1.0, 0.0), axis=0, keepdims=True)
        total = jnp.sum(total, axis=1, keepdims=True)
        start = start + jnp.where(q_seg > rollout, total, 0.0)
    start = start.astype(jnp.int32)
    sub = lax.broadcasted_iota(jnp.int32, (SHARE, rows), 0)
    latest = q_pos - sub
    earliest = start - sub
    for block in range(ctx):
        base = order[block] * rows + class_part[block // zs] * SHARE
        seen = (latest >= base) & (earliest <= base)
        bias[pl.ds(block * SHARE, SHARE), :] = jnp.where(seen, 0.0, NEG_FILL)

    loads[7].wait()
    loads[8].wait()
    heads = [pl.ds(h * hd, hd) for h in range(HEADS)]
    lanes = [pl.ds(h * rows, rows) for h in range(HEADS)]
    q_rows = jnp.concatenate([q_in[:, cols] for cols in heads], axis=0)
    do_rows = jnp.concatenate([do_in[:, cols] for cols in heads], axis=0)
    drain(kv.at[most], recv_sem.at[KV])
    wide = kv[...].astype(F32)
    key = wide[:, :SHARE, :].reshape(keys, hd).astype(BF)
    value = wide[:, SHARE:, :].reshape(keys, hd).astype(BF)
    expo[...] = contract(key, q_rows, ((1,), (1,)))
    dprob[...] = contract(value, do_rows, ((1,), (1,)))
    for h in range(HEADS):
        scores = expo[:, lanes[h]] * scale + bias[...]
        top = jnp.max(scores, axis=0, keepdims=True)
        weights = jnp.exp(scores - top)
        expo[:, lanes[h]] = weights
        total = jnp.sum(weights, axis=0, keepdims=True)
        tops[h : h + 1] = top
        stats[r, 0, h : h + 1] = top + jnp.log(total)
        stats[r, 1, h : h + 1] = (
            jnp.sum(weights * dprob[:, lanes[h]], axis=0, keepdims=True) / total
        )
    tops[HEADS:] = jnp.zeros((8 - HEADS, rows), F32)
    for i in range(2):
        stats[r, i, HEADS:] = jnp.zeros((8 - HEADS, rows), F32)
    for way, y, x, core in at.across((4, 0)):
        if way != (0, 0, 0):
            send(stats.at[r], stats.at[r], sems, STATS, at.device(y, at.z, x, core))
    drain(stats.at[others], recv_sem.at[STATS])
    top = jnp.max(stats[:, 0], axis=0)
    factor = jnp.exp(stats[:, 0] - top[None])
    total = jnp.sum(factor, axis=0)
    delta = jnp.sum(stats[:, 1] * factor, axis=0) / total
    norm = jnp.exp(tops[...] - top) / total

    probs, dscores = [], []
    for h in range(HEADS):
        prob = expo[:, lanes[h]] * norm[h : h + 1]
        dscores.append((prob * (dprob[:, lanes[h]] - delta[h : h + 1])).astype(BF))
        probs.append(prob.astype(BF))
    dscore = jnp.concatenate(dscores, axis=1)
    key_grad = contract(dscore, q_rows, ((1,), (0,))) * scale
    value_grad = contract(jnp.concatenate(probs, axis=1), do_rows, ((1,), (0,)))
    both = jnp.concatenate(
        [key_grad.reshape(ctx, SHARE, hd), value_grad.reshape(ctx, SHARE, hd)], axis=1
    )
    dkv_to[...] = both.astype(BF)

    back = at.turn(-2)
    back_block = at.block(back, at.z)
    back_part = at.part(back)

    def scatter(to, arrived, which):
        for dy, dz in at.window((2, 1, 0, -1)):
            z = at.around_z(dz)
            if (dy, dz) != (0, 0):
                home = at.block(at.turn(dy - 2), z)
                send(to.at[home], arrived.at[c], sems, which, at.device(at.turn(dy), z))
        arrived[c] = to[back_block]

    scatter(dkv_to, dkv_from, DKV)

    drain(dkv_from.at[most], recv_sem.at[DKV])
    kvg_own[...] = jnp.sum(dkv_from[...].astype(F32), axis=0).astype(BF)

    def spread(own, arrived, which):
        for _, y, x, core in at.across((2, -2)):
            send(own, arrived.at[back_part], sems, which, at.device(y, at.z, x, core))

    spread(kvg_own, kvg, KVG)

    dq_to[...] = contract(dscore, key, ((0,), (0,))).astype(BF)
    sibling = at.device(at.y, at.z, at.x, 1 - at.core)
    side = dq_half.shape[0]

    def half(core):
        return pl.ds(pl.multiple_of(core * side, 16), side)

    def slot(y, x):
        return x * 2 + lax.div(y, RUN)

    def dq_piece(number):
        return pl.ds(pl.multiple_of(number * piece, 16), piece)

    mine = slot(at.y, at.x)
    chips = [(y, x) for way, y, x, _ in at.across((4, 0)) if way[2] == 0 and way != (0, 0, 0)]
    send(dq_to.at[half(1 - at.core)], dq_near, sems, PAIR, sibling)
    drain(dq_near, recv_sem.at[PAIR])
    dq_half[...] = (dq_to[half(at.core)].astype(F32) + dq_near[...].astype(F32)).astype(BF)
    for y, x in chips:
        send(dq_half.at[dq_piece(slot(y, x))], dq_from.at[mine], sems, DQ, at.device(y, at.z, x))
    dq_from[mine] = dq_half[dq_piece(mine)]

    for load in loads[9:]:
        load.wait()
    drain(kvg, recv_sem.at[KVG])
    wide = kvg[...].astype(F32)
    kv_wide[0] = wide[:, :SHARE, :].reshape(rows, hd)
    kv_wide[1] = wide[:, SHARE:, :].reshape(rows, hd)
    key_grad = kv_wide[0].astype(BF)
    product = contract(x_in[...].reshape(ctx * OWN, rows), key_grad, ((1,), (0,)))
    wg_to[...] = product.astype(BF).reshape(ctx, OWN, hd)
    scatter(wg_to, wg_from, WG)

    kvg_stage[:, :hd] = key_grad
    kvg_stage[:, hd:] = kv_wide[1].astype(BF)
    outs = []

    def put(src, dst):
        outs.append(pltpu.make_async_copy(src, dst, out_sem.at[len(outs)]))
        outs[-1].start()

    put(kvg_stage, kvg_out)
    drain(dq_from.at[pl.ds(0, len(chips))], recv_sem.at[DQ])
    dq_side[dq_piece(mine)] = (jnp.sum(dq_from[...].astype(F32), axis=0) * scale).astype(BF)
    summed = dq_side.at[dq_piece(mine)]
    for y, x in chips:
        send(summed, summed, sems, DQALL, at.device(y, at.z, x))

    drain(state, recv_sem.at[STATE])
    drain(wg_from.at[most], recv_sem.at[WG])
    grad = jnp.sum(wg_from[...].astype(F32), axis=0)
    master = state[0]
    new_first = BETA_ONE * state[1] + (1.0 - BETA_ONE) * grad
    new_second = BETA_TWO * state[2] + (1.0 - BETA_TWO) * grad * grad
    update = (
        new_first / CORRECT_ONE / (jnp.sqrt(new_second / CORRECT_TWO) + ADAM_EPS)
        + DECAY_RATE * master
    )
    new_master = master - LEARN_RATE * update
    rolled_own[...] = new_master.astype(BF)
    spread(rolled_own, rw_out, ROLL)
    state_new[0] = new_master
    state_new[1] = new_first
    state_new[2] = new_second
    for i, out in enumerate((mw_out, m1_out, m2_out)):
        send(state_new.at[i], out, sems, BACK, at.device(back, at.z))

    dq_most = pl.ds(0, len(chips) * piece)
    drain(dq_side.at[dq_most], recv_sem.at[DQALL])
    send(dq_side, qg_out.at[half(at.core)], sems, GIVE, sibling)
    put(dq_side, qg_out.at[half(at.core)])
    drain(kv.at[most], send_sem.at[KV])
    drain(state_in, send_sem.at[STATE])
    drain(stats.at[others], send_sem.at[STATS])
    drain(dkv_to.at[most], send_sem.at[DKV])
    drain(dq_near, send_sem.at[PAIR])
    drain(dq_side.at[dq_most], send_sem.at[DQ])
    drain(kvg, send_sem.at[KVG])
    drain(wg_to.at[most], send_sem.at[WG])
    drain(dq_side.at[dq_most], send_sem.at[DQALL])
    drain(dq_side, send_sem.at[GIVE])
    drain(kvg, send_sem.at[ROLL])
    drain(state_new, send_sem.at[BACK])
    drain(state_new, recv_sem.at[BACK])
    drain(dq_side, recv_sem.at[GIVE])
    drain(kvg, recv_sem.at[ROLL])
    for out in outs:
        out.wait()


def hand_over(*refs):
    sources, places, held, sem = refs[:6], refs[6:12], refs[12:18], refs[18]
    rows, hd = places[0].shape[0], sources[0].shape[1]
    moves = []
    for h in range(HEADS):
        span = pl.ds(h * rows, rows)
        moves.append((sources[0].at[span], held[0].at[span], places[0].at[:, pl.ds(h * hd, hd)]))
    moves += list(zip(sources[1:], held[1:], places[1:]))
    fetches = [
        pltpu.make_async_copy(src, mid, sem.at[0, n]) for n, (src, mid, _) in enumerate(moves)
    ]
    writes = [
        pltpu.make_async_copy(mid, dst, sem.at[1, n]) for n, (_, mid, dst) in enumerate(moves)
    ]
    for fetch in fetches:
        fetch.start()
    for fetch, write in zip(fetches, writes):
        fetch.wait()
        write.start()
    for write in writes:
        write.wait()


def body(order, segments, layer_input, query, key, value, out_grad, master, first, second):
    ctx = lax.axis_size("ctx")
    roll = lax.axis_size("roll")
    rows, hd = key.shape
    width = query.shape[1]
    keys = ctx * SHARE
    piece = HEADS * SHARE
    shape = jax.ShapeDtypeStruct
    vmem = pltpu.VMEM
    anywhere = pl.BlockSpec(memory_space=pl.ANY)
    shapes = (
        shape((rows, width), BF),
        shape((rows, 2 * hd), BF),
        shape((OWN, hd), F32),
        shape((OWN, hd), F32),
        shape((OWN, hd), F32),
        shape((roll, OWN, hd), BF),
    )
    made = pl.pallas_call(
        functools.partial(kernel, ctx, roll),
        out_shape=(shape((HEADS * rows, hd), BF), *shapes[1:]),
        in_specs=[anywhere] * 10,
        out_specs=[anywhere] * 6,
        scratch_shapes=[
            pltpu.SMEM((ctx,), jnp.int32),
            vmem((ctx, rows), jnp.int32),
            vmem((ctx, OWN, rows), BF),
            vmem((rows, width), BF),
            vmem((rows, hd), BF),
            vmem((rows, hd), BF),
            vmem((rows, width), BF),
            vmem((3, OWN, hd), F32),
            vmem((3, OWN, hd), F32),
            vmem((3, OWN, hd), F32),
            vmem((2, rows, hd), F32),
            vmem((keys, rows), F32),
            vmem((keys, HEADS * rows), F32),
            vmem((keys, HEADS * rows), F32),
            vmem((ctx, 2 * SHARE, hd), BF),
            vmem((2 * SHARE, hd), BF),
            vmem((8, rows), F32),
            vmem((roll, 2, 8, rows), F32),
            vmem((ctx, 2 * SHARE, hd), BF),
            vmem((ctx, 2 * SHARE, hd), BF),
            vmem((roll * piece, hd), BF),
            vmem((roll // 2 * piece, hd), BF),
            vmem((roll // 2 * piece, hd), BF),
            vmem((roll // 2, piece, hd), BF),
            vmem((roll // 2 * piece, hd), BF),
            vmem((roll, 2 * SHARE, hd), BF),
            vmem((2 * SHARE, hd), BF),
            vmem((ctx, OWN, hd), BF),
            vmem((ctx, OWN, hd), BF),
            vmem((OWN, hd), BF),
            vmem((rows, 2 * hd), BF),
            pltpu.SemaphoreType.DMA((13,)),
            pltpu.SemaphoreType.DMA((12,)),
            pltpu.SemaphoreType.DMA((12,)),
            pltpu.SemaphoreType.DMA((12,)),
        ],
        compiler_params=pltpu.CompilerParams(
            collective_id=0, has_side_effects=True, vmem_limit_bytes=56 * 1024 * 1024
        ),
    )(
        order,
        segments.reshape(ctx, rows),
        layer_input.reshape(ctx, roll, OWN, rows),
        query,
        key,
        value,
        out_grad,
        master,
        first,
        second,
    )
    query_grad, key_value, new_master, new_first, new_second, rolled = pl.pallas_call(
        hand_over,
        out_shape=shapes,
        in_specs=[anywhere] * 6,
        out_specs=[anywhere] * 6,
        scratch_shapes=[
            vmem((HEADS * rows, hd), BF),
            *(vmem(s.shape, s.dtype) for s in shapes[1:]),
            pltpu.SemaphoreType.DMA((2, 11)),
        ],
    )(*made)
    return (
        query_grad,
        key_value,
        new_master,
        new_first,
        new_second,
        rolled.reshape(roll * OWN, hd),
    )


def solution(mesh):
    placed = (
        P(),
        P(),
        P(None, "ctx"),
        P("ctx", None),
        P("ctx", None),
        P("ctx", None),
        P("ctx", None),
        P(("ctx", "roll"), None),
        P(("ctx", "roll"), None),
        P(("ctx", "roll"), None),
    )
    return jax.shard_map(
        body,
        mesh=mesh,
        in_specs=placed,
        out_specs=(
            P("ctx", None),
            P("ctx", None),
            P(("ctx", "roll"), None),
            P(("ctx", "roll"), None),
            P(("ctx", "roll"), None),
            P("ctx", None),
        ),
        check_vma=False,
    )
```
